256 devices in a mesh: dp: 4 (over y), expert: 8 (over z), tensor: 8 (over x, core).
Axes of the slice: x: 4, y: 4, z: 8, core: 2. Of those that a mesh axis runs over, the one named last changes fastest.
Arguments:
- resid: bfloat16 [4, 1024, 3072], P('dp', 'expert'), may hold values from -6 to 6
- queries: bfloat16 [4, 1024, 3072], P('dp', 'expert', 'tensor'), may hold values from -42 to 42
- keys: bfloat16 [4, 1024, 1024], P('dp', 'expert', 'tensor'), may hold values from -7 to 7
- values: bfloat16 [4, 1024, 1024], P('dp', 'expert', 'tensor'), may hold values from -6 to 6
- out_weight: bfloat16 [3072, 3072], P('tensor', ('dp', 'expert')), may hold values from -0.109375 to 0.109375
- norm_gain: float32 [3072], replicated, may hold values from 0.25 to 1.75
- router_weight: bfloat16 [3072, 8], replicated, may hold values from -0.109375 to 0.109375
- gate_weight: bfloat16 [8, 3072, 5376], P('expert', None, 'tensor'), may hold values from -0.109375 to 0.109375
- up_weight: bfloat16 [8, 3072, 5376], P('expert', None, 'tensor'), may hold values from -0.109375 to 0.109375
- down_weight: bfloat16 [8, 5376, 3072], P('expert', 'tensor'), may hold values from -0.078125 to 0.078125
- expert_ids: int32 [4, 1024, 4], P('dp', 'expert'), may hold values from 0 to 7, all different within a row; in each aligned block of 128 rows (0 to 127, 128 to 255, ..., all dimensions but the last counted through in order) at most 80 rows name the same one
Outputs:
- block_out: bfloat16 [4, 1024, 3072], P('dp', ('expert', 'tensor'))
The draws below stay inside these ranges and needn't reach their ends.
Inputs may be any that keep to these rules, and one draw needn't show every extreme that they name: `expert_ids`: each row names 4 different experts; in every aligned block of 128 rows in order (sequence, position) no expert is named by more than 80 rows, and in some blocks one is named by exactly 80.
All inputs are finite; a program needn't handle non-finite values.
Results may differ from the reference program's by a relative error of at most 0.015.
Values may be sent and summed in bfloat16 or wider, within the bound.
A program may use at most 128 MiB of HBM per device.

```python
import math
import jax
import jax.numpy as jnp
import numpy as np
from jax import lax

D = 3072
HEADS = 24
KV_HEADS = 8
HEAD_WIDTH = 128
FF = 5376
EXPERTS = 8
TOP = 4
ROWS = 128
CAP = 80
SEQ = 1024
BATCH = 4
N_TENSOR = 8


def shared_normal(key, spread, limit):
    return jnp.clip(spread * jax.random.normal(key, (BATCH, SEQ, KV_HEADS, HEAD_WIDTH), jnp.float32), -limit, limit)


def draw_keys(key, part):
    core = shared_normal(key, 1.2, 7.0)
    return core.reshape(BATCH, SEQ, KV_HEADS * HEAD_WIDTH).astype(jnp.bfloat16)


def draw_queries(key, part):
    key = jax.random.fold_in(key, 9)
    drawn = jnp.clip(1.2 * jax.random.normal(key, (BATCH, SEQ, HEADS, HEAD_WIDTH), jnp.float32), -7.0, 7.0)
    return drawn.reshape(BATCH, SEQ, HEADS * HEAD_WIDTH).astype(jnp.bfloat16)


def steps_of(rng, extent, split, least, largest):
    factor_of = 1.0
    for axis_at, parts in split:
        steps = jax.random.uniform(jax.random.fold_in(jax.random.fold_in(rng, 6), axis_at), (parts,), jnp.float32, least / len(split), largest / len(split))
        factor_of = factor_of * jnp.repeat(jnp.exp(steps), extent[axis_at] // parts).reshape((-1,) + (1,) * (len(extent) - 1 - axis_at))
    return factor_of


def shared_out(rng, own, number, rows, number_of, top, bound, lean):
    sequence = jax.random.permutation(rng, number_of)
    heavy_load, ordinary = portions_of(number_of, rows * top, bound, lean, True), portions_of(number_of, rows * top, bound, lean, False)
    places = jnp.arange(number_of)

    def named(lengths, turn):
        used = int((lengths > 0).sum())
        fixed = max(1, used // 4)
        shifted = fixed + (places - fixed + turn * (used - fixed)) % max(1, number_of - fixed)
        return jnp.zeros((number_of,), jnp.int32).at[sequence[jnp.where(places < fixed, places, shifted)]].set(jnp.asarray(lengths, jnp.int32))

    lengths = jnp.where(number % 4 == 0, named(heavy_load, number // 4), named(ordinary, number - number // 4 - 1))
    mixed = jax.random.permutation(jax.random.fold_in(own, 3), number_of)
    donor, receiver = mixed[0:number_of // 2 * 2:2], mixed[1:number_of // 2 * 2:2]
    margin = jnp.minimum(lengths[donor] - 1, bound - lengths[receiver]) // 2
    margin = jnp.where((donor == sequence[0]) | (receiver == sequence[0]) | (lengths[receiver] == 0), 0, jnp.maximum(margin, 0))
    shifted = jax.random.randint(jax.random.fold_in(own, 4), (number_of // 2,), 0, 1 << 20) % (margin + 1)
    lengths = lengths.at[donor].add(-shifted).at[receiver].add(shifted)
    items = jnp.searchsorted(jnp.cumsum(lengths), jnp.arange(rows * top), side="right").astype(jnp.int32)
    listing = items.reshape(top, rows).T
    listing = listing[jax.random.permutation(jax.random.fold_in(own, 1), rows)]
    turn = jax.random.randint(jax.random.fold_in(own, 2), (rows, 1), 0, top)
    return jnp.take_along_axis(listing, (jnp.arange(top)[None, :] + turn) % top, axis=1)


def portions_of(number_of, total, most, lean, full):
    portions = [(1 << 20) // math.isqrt(rank ** lean) + 1 for rank in range(1, number_of + 1)]
    largest = most if full else min(most, max(-(-total // number_of), total * portions[0] // sum(portions)))
    least = 1 if total - largest >= number_of - 1 else 0
    given, rest = [largest] + [least] * (number_of - 1), total - largest - least * (number_of - 1)
    while rest > 0:
        free = [i for i in range(1, number_of) if given[i] < largest] or [i for i in range(1, number_of) if given[i] < most]
        whole, budget = sum([portions[i] for i in free]), rest
        for i in free:
            more = min(most - given[i], max(1, budget * portions[i] // whole), rest)
            given[i] = given[i] + more
            rest = rest - more
    return np.array(given)


def scatter_about(key, extent, scale, reach, split=(), kind=jnp.bfloat16):
    values = jax.random.normal(key, extent, jnp.float32) * scale
    if len(split) > 0:
        values = steps_of(key, extent, split, -0.22, 0.18) * values
    return jnp.clip(values, min=-reach, max=reach).astype(kind)


def setup_inputs(seed: int = 0) -> dict:
    arg_keys = jax.random.split(jax.random.key(seed), 12)
    resid = scatter_about(arg_keys[0], (BATCH, SEQ, D), 1.0, 6.0, ((0, 4), (1, 8)))
    queries = draw_queries(jax.random.fold_in(arg_keys[11], 71), 0)
    keys = draw_keys(jax.random.fold_in(arg_keys[11], 71), 0)
    values = scatter_about(arg_keys[3], (BATCH, SEQ, KV_HEADS * HEAD_WIDTH), 1.0, 6.0, ((0, 4), (1, 8), (2, 8)))
    out_weight = scatter_about(arg_keys[4], (HEADS * HEAD_WIDTH, D), (HEADS * HEAD_WIDTH) ** -0.5, 0.109375, ((0, 8), (1, 32)))
    norm_gain = jnp.clip(1.0 + 0.15 * jax.random.normal(arg_keys[5], (D,), jnp.float32), 0.25, 1.75)
    router_weight = scatter_about(arg_keys[6], (D, EXPERTS), D ** -0.5, 0.109375)
    gate_weight = scatter_about(arg_keys[7], (EXPERTS, D, FF), D ** -0.5, 0.109375, ((0, 8), (2, 8)))
    up_weight = scatter_about(arg_keys[8], (EXPERTS, D, FF), D ** -0.5, 0.109375, ((0, 8), (2, 8)))
    down_weight = scatter_about(arg_keys[9], (EXPERTS, FF, D), FF ** -0.5, 0.078125, ((0, 8), (1, 8)))
    expert_ids_keys = jax.random.split(jax.random.fold_in(arg_keys[10], 1), BATCH * SEQ // ROWS)
    expert_ids_turns = jax.random.permutation(jax.random.fold_in(arg_keys[10], 3), BATCH * SEQ // ROWS)
    expert_ids = jax.vmap(lambda own, number: shared_out(jax.random.fold_in(arg_keys[10], 2), own, number, ROWS, EXPERTS, TOP, CAP, 2))(expert_ids_keys, expert_ids_turns).reshape((BATCH, SEQ, TOP))
    return {"resid": resid, "queries": queries, "keys": keys, "values": values, "out_weight": out_weight, "norm_gain": norm_gain, "router_weight": router_weight, "gate_weight": gate_weight, "up_weight": up_weight, "down_weight": down_weight, "expert_ids": expert_ids}


def attend(queries, keys, values):
    head_ratio = HEADS // KV_HEADS
    query_all = queries.reshape(BATCH, SEQ, HEADS, HEAD_WIDTH).astype(jnp.float32)
    key_all = keys.reshape(BATCH, SEQ, KV_HEADS, HEAD_WIDTH).astype(jnp.float32)
    value_all = values.reshape(BATCH, SEQ, KV_HEADS, HEAD_WIDTH).astype(jnp.float32)
    positions = jnp.arange(SEQ, dtype=jnp.int32)
    causal = positions[None, :] <= positions[:, None]

    def one_head(head_index):
        query_per_head = lax.dynamic_index_in_dim(query_all, head_index, 2, keepdims=False)
        key_per_head = lax.dynamic_index_in_dim(key_all, head_index // head_ratio, 2, keepdims=False)
        value_per_head = lax.dynamic_index_in_dim(value_all, head_index // head_ratio, 2, keepdims=False)
        score_matrix = jnp.einsum('urg,ulg->url', query_per_head, key_per_head) * HEAD_WIDTH ** (-0.5)
        score_matrix = jnp.where(causal[None], score_matrix, -jnp.inf)
        weight_matrix = jax.nn.softmax(score_matrix, axis=-1).astype(jnp.bfloat16)
        return jnp.einsum('vzx,vxy->vzy', weight_matrix.astype(jnp.float32), value_per_head).astype(jnp.bfloat16)
    per_head = lax.map(one_head, jnp.arange(HEADS, dtype=jnp.int32))
    return jnp.transpose(per_head, (1, 2, 0, 3)).reshape(BATCH * SEQ, HEADS * HEAD_WIDTH)

def run_expert(pieces):
    slot_rows, w_gate, w_up, w_down = pieces
    gate_act = jnp.dot(slot_rows, w_gate, preferred_element_type=jnp.float32)
    up_act = jnp.dot(slot_rows, w_up, preferred_element_type=jnp.float32)
    hidden = (jax.nn.silu(gate_act) * up_act).astype(jnp.bfloat16)
    slice_width = FF // N_TENSOR
    summed = jnp.zeros((slot_rows.shape[0], D), jnp.float32)
    for group_index in range(N_TENSOR):
        low = group_index * slice_width
        partial_term = jnp.dot(hidden[:, low:low + slice_width], w_down[low:low + slice_width], preferred_element_type=jnp.float32).astype(jnp.bfloat16)
        summed = summed + lax.optimization_barrier(partial_term).astype(jnp.float32)
    return summed.astype(jnp.bfloat16)

def reference(resid, queries, keys, values, out_weight, norm_gain, router_weight, gate_weight, up_weight, down_weight, expert_ids):
    rows_all = BATCH * SEQ
    heads_out = attend(queries, keys, values)
    attention = jnp.dot(heads_out, out_weight, preferred_element_type=jnp.float32)
    mixed = resid.reshape(rows_all, D).astype(jnp.float32) + attention
    mean_square = lax.optimization_barrier(jnp.mean(mixed * mixed, axis=-1, keepdims=True))
    normed = (mixed * lax.rsqrt(mean_square + 1e-05) * norm_gain).astype(jnp.bfloat16)
    logits = jnp.dot(normed, router_weight, preferred_element_type=jnp.float32)
    chosen = expert_ids.reshape(rows_all, TOP).astype(jnp.int32)
    gate_scores_topk = jax.nn.sigmoid(jnp.take_along_axis(logits, chosen, axis=1))
    blocks = rows_all // ROWS
    flat_ids = chosen.reshape(blocks, ROWS * TOP)
    onehot = (flat_ids[:, :, None] == jnp.arange(EXPERTS, dtype=jnp.int32)[None, None, :]).astype(jnp.int32)
    before = jnp.cumsum(onehot, axis=1) - onehot
    slot_index = lax.optimization_barrier(jnp.sum(before * onehot, axis=2)).astype(jnp.int32)
    position = (jnp.arange(blocks, dtype=jnp.int32)[:, None] * EXPERTS + flat_ids) * CAP + slot_index
    slot_flat = position.reshape(rows_all * TOP).astype(jnp.int32)
    source = jnp.repeat(normed, TOP, axis=0)
    slot_table = jnp.zeros((blocks * EXPERTS * CAP, D), jnp.bfloat16).at[slot_flat].set(source)
    slot_table = jnp.transpose(slot_table.reshape(blocks, EXPERTS, CAP, D), (1, 0, 2, 3)).reshape(EXPERTS, blocks * CAP, D)
    results = lax.map(run_expert, (slot_table, gate_weight, up_weight, down_weight))
    results = jnp.transpose(results.reshape(EXPERTS, blocks, CAP, D), (1, 0, 2, 3)).reshape(blocks * EXPERTS * CAP, D)
    picked = results[slot_flat].reshape(rows_all, TOP, D).astype(jnp.float32)
    expert_mix = lax.optimization_barrier(jnp.sum(gate_scores_topk[:, :, None] * picked, axis=1))
    return (mixed + expert_mix).astype(jnp.bfloat16).reshape(BATCH, SEQ, D)
```

```python
import functools

import jax
import jax.numpy as jnp
from jax import lax
from jax.experimental import pallas as pl
from jax.experimental.pallas import tpu as pltpu
from jax.sharding import PartitionSpec as P

HEAD_WIDTH = 128
CAP = 80
MESH = pl.DeviceIdType.MESH
F32 = jnp.float32
BF16 = jnp.bfloat16
NT = (((1,), (1,)), ((), ()))


def remote(src, dst, send_sem, recv_sem, device):
    return pltpu.make_async_remote_copy(
        src_ref=src,
        dst_ref=dst,
        send_sem=send_sem,
        recv_sem=recv_sem,
        device_id=device,
        device_id_type=MESH,
    )


def greet(devices):
    barrier = pltpu.get_barrier_semaphore()
    for device in devices:
        pl.semaphore_signal(barrier, inc=1, device_id=device, device_id_type=MESH)
    pl.semaphore_wait(barrier, len(devices))


def attention_kernel(
    n_y, n_z, n_t,
    q_ref, k_ref, v_ref, w_ref, resid_ref, gain_ref, router_ref,
    mixed_ref, cols_ref, logit_ref,
    kv, w, scores, heads, part, peer, sums, cross, att, attn, res, sendn,
    kv_ss, kv_rs, w_ss, w_rs, h_ss, h_rs, p_ss, p_rs, x_ss, x_rs, y_ss, y_rs,
    n_ss, n_rs, l_ss, l_rs, res_sem,
):
    n_x = n_t // 2
    y, z, t = lax.axis_index("dp"), lax.axis_index("expert"), lax.axis_index("tensor")
    x, c = lax.div(t, 2), lax.rem(t, 2)
    right, left = lax.rem(z + 1, n_z), lax.rem(z + n_z - 1, n_z)
    rows = q_ref.shape[0]
    group = q_ref.shape[1] // HEAD_WIDTH
    width = mixed_ref.shape[1]
    ycols, tcols, trows = width // n_y, width // n_t, rows // n_t
    per = n_t // n_y
    half = w_ref.shape[0] // 2

    res_copy = pltpu.make_async_copy(
        resid_ref.at[pl.ds(pl.multiple_of(t * trows, trows), trows)], res, res_sem
    )
    res_copy.start()
    kv[z, 0] = k_ref[...]
    kv[z, 1] = v_ref[...]
    w[z] = w_ref[...]
    greet(
        [{"expert": right}, {"expert": left}]
        + [{"dp": lax.rem(y + d, n_y)} for d in range(1, n_y)]
        + [{"tensor": lax.rem(t + d, n_t)} for d in range(1, n_t)]
    )

    hops = n_z // 2

    def kv_hop(way, s):
        block = lax.rem(z + (n_z - s if way == 0 else s), n_z)
        ref = kv.at[block, way] if s == hops - 1 else kv.at[block]
        return remote(
            ref, ref, kv_ss.at[way, s], kv_rs.at[way, s], {"expert": right if way == 0 else left}
        )

    def w_hop(way, s):
        block = lax.rem(z + (n_z - s if way == 0 else s), n_z)
        ref = w.at[block, pl.ds(way * half, half)] if s == hops - 1 else w.at[block]
        return remote(
            ref, ref, w_ss.at[way, s], w_rs.at[way, s], {"expert": right if way == 0 else left}
        )

    def score(block):
        for h in range(group):
            scores[block, h] = lax.dot_general(
                q_ref[:, h * HEAD_WIDTH : (h + 1) * HEAD_WIDTH],
                kv[block, 0],
                NT,
                preferred_element_type=F32,
            )

    for s in range(hops):
        for way in range(2):
            if s > 0:
                kv_hop(way, s - 1).wait_recv()
            kv_hop(way, s).start()
        for way in range(2):
            if s > 0:
                w_hop(way, s - 1).wait_recv()
            w_hop(way, s).start()
        score(lax.rem(z + n_z - s, n_z))
        if s > 0:
            score(lax.rem(z + s, n_z))
    for way in range(2):
        kv_hop(way, hops - 1).wait_recv()
    score(lax.rem(z + hops, n_z))

    all_values = kv[:, 1].reshape(n_z * rows, HEAD_WIDTH)
    shape = (rows, n_z * rows)
    causal = lax.broadcasted_iota(jnp.int32, shape, 1) <= (
        lax.broadcasted_iota(jnp.int32, shape, 0) + z * rows
    )
    for h in range(group):
        s_h = jnp.concatenate([scores[b, h] for b in range(n_z)], axis=1) * HEAD_WIDTH ** (-0.5)
        s_h = jnp.where(causal, s_h, -jnp.inf)
        e_h = jnp.exp(s_h - jnp.max(s_h, axis=1, keepdims=True))
        a_h = (e_h * (1.0 / jnp.sum(e_h, axis=1, keepdims=True))).astype(BF16)
        o_h = jnp.dot(a_h, all_values, preferred_element_type=F32)
        heads[y, :, h * HEAD_WIDTH : (h + 1) * HEAD_WIDTH] = o_h.astype(BF16)

    def heads_copy(d):
        return remote(
            heads.at[y], heads.at[y], h_ss.at[d - 1], h_rs.at[d - 1], {"dp": lax.rem(y + d, n_y)}
        )

    for d in range(1, n_y):
        heads_copy(d).start()
    for way in range(2):
        w_hop(way, hops - 1).wait_recv()

    sibling = {"tensor": t + 1 - 2 * c}
    w_all = w[...].reshape(ycols, w.shape[2])

    def pair_copy(j):
        g = lax.rem(y + n_y - j, n_y)
        return remote(part.at[1 - c, g], peer.at[g], p_ss.at[j], p_rs.at[j], sibling)

    for j in range(n_y):
        g = lax.rem(y + n_y - j, n_y)
        if j > 0:
            heads_copy(j).wait_recv()
        pr = lax.dot_general(heads[g], w_all, NT, preferred_element_type=F32)
        pr = pr.astype(BF16).reshape(n_x, 2, trows, ycols)
        part[0, g] = pr[:, 0]
        part[1, g] = pr[:, 1]
        pair_copy(j).start()
    for j in range(n_y):
        g = lax.rem(y + n_y - j, n_y)
        pair_copy(j).wait_recv()
        sums[:, g] = (part[c, g].astype(F32) + peer[g].astype(F32)).astype(BF16)

    def cross_copy(d):
        to = lax.rem(x + d, n_x)
        return remote(
            sums.at[to], cross.at[d - 1], x_ss.at[d - 1], x_rs.at[d - 1], {"tensor": to * 2 + c}
        )

    for d in range(1, n_x):
        cross_copy(d).start()
    total = sums[x].astype(F32)
    for d in range(1, n_x):
        cross_copy(d).wait_recv()
        total = total + cross[d - 1].astype(F32)
    att[...] = total.astype(BF16)

    def back_copy(d):
        to = lax.rem(y + d, n_y)
        return remote(att.at[to], attn.at[y], y_ss.at[d - 1], y_rs.at[d - 1], {"dp": to})

    for d in range(1, n_y):
        back_copy(d).start()
    attn[y] = att[y]
    res_copy.wait()
    for d in range(1, n_y):
        back_copy(d).wait_recv()

    mixed = []
    square = jnp.zeros((trows, 1), F32)
    for g in range(n_y):
        m_g = res[:, g * ycols : (g + 1) * ycols].astype(F32) + attn[g].astype(F32)
        mixed_ref[:, g * ycols : (g + 1) * ycols] = m_g
        square = square + jnp.sum(m_g * m_g, axis=1, keepdims=True)
        mixed.append(m_g)
    scale = lax.rsqrt(square * (1.0 / width) + 1e-05)
    logits = None
    for g in range(n_y):
        normed = (mixed[g] * scale * gain_ref[:, g * ycols : (g + 1) * ycols]).astype(BF16)
        for i in range(per):
            sendn[g * per + i] = normed[:, i * tcols : (i + 1) * tcols]
        term = lax.dot_general(
            normed,
            router_ref[:, g * ycols : (g + 1) * ycols],
            NT,
            preferred_element_type=F32,
        )
        logits = term if logits is None else logits + term
    lane = lax.broadcasted_iota(jnp.int32, (trows, 128), 1)
    wide = jnp.zeros((trows, 128), F32)
    for e in range(router_ref.shape[0]):
        wide = jnp.where(lane == e, logits[:, e : e + 1], wide)
    logit_ref[t] = wide
    cols_ref[t] = sendn[t]

    def cols_copy(d):
        to = lax.rem(t + d, n_t)
        return remote(
            sendn.at[to], cols_ref.at[t], n_ss.at[d - 1], n_rs.at[d - 1], {"tensor": to}
        )

    def logit_copy(d):
        to = lax.rem(t + d, n_t)
        return remote(
            logit_ref.at[t], logit_ref.at[t], l_ss.at[d - 1], l_rs.at[d - 1], {"tensor": to}
        )

    for d in range(1, n_t):
        cols_copy(d).start()
        logit_copy(d).start()
    for d in range(1, n_t):
        cols_copy(d).wait_recv()
        logit_copy(d).wait_recv()

    for way in range(2):
        for s in range(hops):
            kv_hop(way, s).wait_send()
            w_hop(way, s).wait_send()
    for d in range(1, n_y):
        heads_copy(d).wait_send()
        back_copy(d).wait_send()
    for j in range(n_y):
        pair_copy(j).wait_send()
    for d in range(1, n_x):
        cross_copy(d).wait_send()
    for d in range(1, n_t):
        cols_copy(d).wait_send()
        logit_copy(d).wait_send()


def expert_kernel(
    n_y, n_z, n_t, order,
    cols_ref, logit_ref, ids_ref, mixed_ref, wg_ref, wu_ref, wd_ref,
    out_ref,
    wg, wu, wd, slots, xbuf, table, hidden, act_g, act_u, part, peer, cross, ybuf, zbuf, comb_hi,
    comb_lo, mix, fin,
    wsem, s_ss, s_rs, a_ss, a_rs, b_ss, b_rs, p_ss, p_rs, x_ss, x_rs, z_ss, z_rs, f_ss, f_rs,
):
    n_x = n_t // 2
    y, z, t = lax.axis_index("dp"), lax.axis_index("expert"), lax.axis_index("tensor")
    x, c = lax.div(t, 2), lax.rem(t, 2)
    rows = ids_ref.shape[1]
    width = mixed_ref.shape[1]
    tcols, trows = width // n_t, rows // n_t
    xcols = width // n_x
    halves = 2
    per_half = n_z // halves
    n_groups = 4 if n_z % 4 == 0 else 2
    per_group = n_z // n_groups
    groups_half = n_groups // halves
    hrows, grows = per_half * CAP, per_group * CAP
    sibling_t = t + 1 - 2 * c

    loads = []
    for i in range(n_x):
        span = pl.ds(i * xcols, xcols)
        loads.append(pltpu.make_async_copy(wg_ref.at[:, span], wg.at[i], wsem.at[0, i]))
        loads.append(pltpu.make_async_copy(wu_ref.at[:, span], wu.at[i], wsem.at[1, i]))
    for i in range(n_x):
        span = pl.ds(i * xcols, xcols)
        loads.append(pltpu.make_async_copy(wd_ref.at[:, span], wd.at[i], wsem.at[2, i]))
    for load in loads:
        load.start()
    greet(
        [{"expert": lax.rem(z + d, n_z)} for d in range(1, n_z)]
        + [{"tensor": lax.rem(t + d, n_t)} for d in range(1, n_t)]
    )

    ids = ids_ref[...]
    n_e = table.shape[0]
    expert = lax.broadcasted_iota(jnp.int32, (n_e, rows), 0)
    named = ids[0:1, :] == expert
    for j in range(1, ids.shape[0]):
        named = jnp.logical_or(named, ids[j : j + 1, :] == expert)
    earlier = (
        lax.broadcasted_iota(jnp.int32, (rows, rows), 0)
        < lax.broadcasted_iota(jnp.int32, (rows, rows), 1)
    )
    before = jnp.dot(
        jnp.where(named, 1.0, 0.0).astype(BF16),
        jnp.where(earlier, 1.0, 0.0).astype(BF16),
        preferred_element_type=F32,
    )
    table[...] = jnp.where(named, before.astype(jnp.int32), -1)
    slot = lax.broadcasted_iota(jnp.int32, (CAP, rows), 0)
    cols = cols_ref[...].reshape(rows, tcols)

    def slot_copy(p):
        to = lax.rem(z + n_z - order[p], n_z)
        return remote(
            slots.at[p],
            xbuf.at[t, pl.ds(p * CAP, CAP)],
            s_ss.at[p],
            s_rs.at[p],
            {"expert": to},
        )

    for p in range(n_z):
        e = lax.rem(z + n_z - order[p], n_z)
        pick = jnp.where(table[pl.ds(e, 1), :] == slot, 1.0, 0.0).astype(BF16)
        picked = jnp.dot(pick, cols, preferred_element_type=F32).astype(BF16)
        if p == 0:
            xbuf[t, 0:CAP] = picked
        else:
            slots[p] = picked
            slot_copy(p).start()

    def share_copy(g, d):
        ref = xbuf.at[t, pl.ds(g * grows, grows)]
        to = lax.rem(x + d, n_x) * 2 + c
        return remote(ref, ref, a_ss.at[g, d - 1], a_rs.at[g, d - 1], {"tensor": to})

    def pass_copy(g, d):
        held = lax.rem(x + n_x - d, n_x) * 2 + c
        ref = xbuf.at[held, pl.ds(g * grows, grows)]
        return remote(ref, ref, b_ss.at[g, d], b_rs.at[g, d], {"tensor": sibling_t})

    def share(g):
        for p in range(g * per_group, (g + 1) * per_group):
            if p > 0:
                slot_copy(p).wait_recv()
        for d in range(1, n_x):
            share_copy(g, d).start()
        pass_copy(g, 0).start()

    def forward(g, d):
        share_copy(g, d).wait_recv()
        pass_copy(g, d).start()

    def arrive(g, d):
        pass_copy(g, d).wait_recv()

    def gate_up(h, d):
        i = lax.rem(x + n_x - d, n_x)
        span = pl.ds(h * hrows, hrows)
        held = jnp.concatenate([xbuf[i * 2, span], xbuf[i * 2 + 1, span]], axis=1)
        g_term = lax.dot_general(held, wg[i], NT, preferred_element_type=F32)
        act_g[...] = g_term if d == 0 else act_g[...] + g_term
        u_term = lax.dot_general(held, wu[i], NT, preferred_element_type=F32)
        act_u[...] = u_term if d == 0 else act_u[...] + u_term

    def pair_copy(h, d):
        i = lax.rem(x + d, n_x)
        return remote(
            part.at[h, 1 - c, i], peer.at[h, i], p_ss.at[h, d], p_rs.at[h, d],
            {"tensor": sibling_t},
        )

    def down(h):
        g_all = act_g[...]
        hidden[...] = (g_all / (1.0 + jnp.exp(-g_all)) * act_u[...]).astype(BF16)
        for d in list(range(1, n_x)) + [0]:
            i = lax.rem(x + d, n_x)
            o = jnp.dot(hidden[...], wd[i], preferred_element_type=F32).astype(BF16)
            part[h, 0, i] = o[:, :tcols]
            part[h, 1, i] = o[:, tcols:]
            pair_copy(h, d).start()

    def cross_copy(h, d):
        to = lax.rem(x + d, n_x)
        return remote(
            part.at[h, c, to], cross.at[h, d - 1], x_ss.at[h, d - 1], x_rs.at[h, d - 1],
            {"tensor": to * 2 + c},
        )

    def reduce_send(h):
        for d in list(range(1, n_x)) + [0]:
            i = lax.rem(x + d, n_x)
            pair_copy(h, d).wait_recv()
            part[h, c, i] = (part[h, c, i].astype(F32) + peer[h, i].astype(F32)).astype(BF16)
            if d > 0:
                cross_copy(h, d).start()

    def return_copy(p):
        to = lax.rem(z + order[p], n_z)
        return remote(
            ybuf.at[p], zbuf.at[pl.ds(p * CAP, CAP)], z_ss.at[p], z_rs.at[p], {"expert": to}
        )

    def reduce_recv(h):
        total = part[h, c, x].astype(F32)
        for d in range(1, n_x):
            cross_copy(h, d).wait_recv()
            total = total + cross[h, d - 1].astype(F32)
        total = total.astype(BF16)
        for i in range(per_half):
            p = h * per_half + i
            block = total[i * CAP : (i + 1) * CAP]
            if p == 0:
                zbuf[0:CAP] = block
            else:
                ybuf[p] = block
                return_copy(p).start()

    def of_half(h):
        return range(h * groups_half, (h + 1) * groups_half)

    for g in range(n_groups):
        share(g)
    gates = jnp.transpose(logit_ref[...].reshape(rows, 128))[0:n_e]
    gates = 1.0 / (1.0 + jnp.exp(-gates))
    pieces = []
    for p in range(n_z):
        e = lax.rem(z + n_z - order[p], n_z)
        pick = jnp.where(expert == e, gates, 0.0)
        pick = jnp.sum(pick, axis=0, keepdims=True)
        pieces.append(jnp.where(table[pl.ds(e, 1), :] == slot, pick, 0.0))
    comb = jnp.transpose(jnp.concatenate(pieces, axis=0))
    high = comb.astype(BF16)
    comb_hi[...] = high
    comb_lo[...] = (comb - high.astype(F32)).astype(BF16)
    for load in loads:
        load.wait()
    for h in range(halves):
        for d in list(range(0, n_x)):
            for g in of_half(h):
                if d > 0:
                    forward(g, d)
            for g in of_half(h):
                arrive(g, d)
            gate_up(h, d)
        down(h)
        reduce_send(h)
    for h in range(halves):
        reduce_recv(h)
    for p in range(1, n_z):
        return_copy(p).wait_recv()

    back = zbuf[...]
    mixture = jnp.dot(comb_hi[...], back, preferred_element_type=F32) + jnp.dot(
        comb_lo[...], back, preferred_element_type=F32
    )
    mix[...] = mixture.astype(BF16).reshape(n_t, trows, tcols)

    def final_copy(d):
        to = lax.rem(t + d, n_t)
        return remote(mix.at[to], fin.at[t], f_ss.at[d - 1], f_rs.at[d - 1], {"tensor": to})

    for d in range(1, n_t):
        final_copy(d).start()
    fin[t] = mix[t]
    for d in range(1, n_t):
        final_copy(d).wait_recv()
    for i in range(n_t):
        span = slice(i * tcols, (i + 1) * tcols)
        out_ref[:, span] = (mixed_ref[:, span] + fin[i].astype(F32)).astype(BF16)

    for p in range(1, n_z):
        slot_copy(p).wait_send()
        return_copy(p).wait_send()
    for g in range(n_groups):
        pass_copy(g, 0).wait_send()
        for d in range(1, n_x):
            share_copy(g, d).wait_send()
            pass_copy(g, d).wait_send()
    for h in range(halves):
        for d in range(n_x):
            pair_copy(h, d).wait_send()
            if d > 0:
                cross_copy(h, d).wait_send()
    for d in range(1, n_t):
        final_copy(d).wait_send()


def slot_order(n_z):
    if n_z == 8:
        return (0, 1, 7, 2, 6, 3, 5, 4)
    return tuple(range(n_z))


def local(
    resid, queries, keys, values, out_weight, norm_gain, router_weight,
    gate_weight, up_weight, down_weight, expert_ids,
):
    n_y, n_z, n_t = lax.axis_size("dp"), lax.axis_size("expert"), lax.axis_size("tensor")
    n_x = n_t // 2
    rows, qcols = queries.shape[1], queries.shape[2]
    width = resid.shape[2]
    ff = gate_weight.shape[2]
    n_e = router_weight.shape[1]
    top = expert_ids.shape[2]
    ycols, tcols, trows, xcols = width // n_y, width // n_t, rows // n_t, width // n_x
    wcols = out_weight.shape[1]
    vmem = pl.BlockSpec(memory_space=pltpu.VMEM)
    hbm = pl.BlockSpec(memory_space=pl.ANY)
    dma = pltpu.SemaphoreType.DMA
    V = pltpu.VMEM
    hops = n_z // 2

    mixed, cols, logits = pl.pallas_call(
        functools.partial(attention_kernel, n_y, n_z, n_t),
        out_shape=(
            jax.ShapeDtypeStruct((trows, width), F32),
            jax.ShapeDtypeStruct((n_t, trows, tcols), BF16),
            jax.ShapeDtypeStruct((n_t, trows, 128), F32),
        ),
        in_specs=[vmem, vmem, vmem, vmem, hbm, vmem, vmem],
        out_specs=(vmem, vmem, vmem),
        scratch_shapes=[
            V((n_z, 2, rows, HEAD_WIDTH), BF16),
            V((n_z, wcols, qcols), BF16),
            V((n_z, qcols // HEAD_WIDTH, rows, rows), F32),
            V((n_y, rows, qcols), BF16),
            V((2, n_y, n_x, trows, ycols), BF16),
            V((n_y, n_x, trows, ycols), BF16),
            V((n_x, n_y, trows, ycols), BF16),
            V((n_x - 1, n_y, trows, ycols), BF16),
            V((n_y, trows, ycols), BF16),
            V((n_y, trows, ycols), BF16),
            V((trows, width), BF16),
            V((n_t, trows, tcols), BF16),
            dma((2, hops)), dma((2, hops)), dma((2, hops)), dma((2, hops)),
            dma((n_y - 1,)), dma((n_y - 1,)), dma((n_y,)), dma((n_y,)),
            dma((n_x - 1,)), dma((n_x - 1,)), dma((n_y - 1,)), dma((n_y - 1,)),
            dma((n_t - 1,)), dma((n_t - 1,)), dma((n_t - 1,)), dma((n_t - 1,)),
            dma,
        ],
        compiler_params=pltpu.CompilerParams(
            collective_id=0, has_side_effects=True, vmem_limit_bytes=40 * 2**20
        ),
    )(
        queries[0], keys[0], values[0], out_weight.T, resid[0], norm_gain[None],
        router_weight.T,
    )

    out = pl.pallas_call(
        functools.partial(expert_kernel, n_y, n_z, n_t, slot_order(n_z)),
        out_shape=jax.ShapeDtypeStruct((trows, width), BF16),
        in_specs=[vmem, vmem, vmem, vmem, hbm, hbm, hbm],
        out_specs=vmem,
        scratch_shapes=[
            V((n_x, ff, xcols), BF16),
            V((n_x, ff, xcols), BF16),
            V((n_x, ff, xcols), BF16),
            V((n_z, CAP, tcols), BF16),
            V((n_t, n_z * CAP, tcols), BF16),
            V((n_e, rows), jnp.int32),
            V((n_z // 2 * CAP, ff), BF16),
            V((n_z // 2 * CAP, ff), F32),
            V((n_z // 2 * CAP, ff), F32),
            V((2, 2, n_x, n_z // 2 * CAP, tcols), BF16),
            V((2, n_x, n_z // 2 * CAP, tcols), BF16),
            V((2, n_x - 1, n_z // 2 * CAP, tcols), BF16),
            V((n_z, CAP, tcols), BF16),
            V((n_z * CAP, tcols), BF16),
            V((rows, n_z * CAP), BF16),
            V((rows, n_z * CAP), BF16),
            V((n_t, trows, tcols), BF16),
            V((n_t, trows, tcols), BF16),
            dma((3, n_x)),
            dma((n_z,)), dma((n_z,)),
            dma((4, n_x - 1)), dma((4, n_x - 1)), dma((4, n_x)), dma((4, n_x)),
            dma((2, n_x)), dma((2, n_x)), dma((2, n_x - 1)), dma((2, n_x - 1)),
            dma((n_z,)), dma((n_z,)), dma((n_t - 1,)), dma((n_t - 1,)),
        ],
        compiler_params=pltpu.CompilerParams(
            collective_id=1, has_side_effects=True, vmem_limit_bytes=56 * 2**20
        ),
    )(
        cols, logits, expert_ids[0].T, mixed,
        jnp.swapaxes(gate_weight, 1, 2)[0], jnp.swapaxes(up_weight, 1, 2)[0], down_weight[0],
    )
    return out[None]


def solution(mesh):
    return jax.shard_map(
        local,
        mesh=mesh,
        in_specs=(
            P("dp", "expert", None),
            P("dp", "expert", "tensor"),
            P("dp", "expert", "tensor"),
            P("dp", "expert", "tensor"),
            P("tensor", ("dp", "expert")),
            P(),
            P(),
            P("expert", None, "tensor"),
            P("expert", None, "tensor"),
            P("expert", "tensor", None),
            P("dp", "expert", None),
        ),
        out_specs=P("dp", ("expert", "tensor"), None),
        check_vma=False,
    )
```

```python
import functools

import jax
import jax.numpy as jnp
from jax import lax
from jax.experimental import pallas as pl
from jax.experimental.pallas import tpu as pltpu
from jax.sharding import PartitionSpec as P

HEAD_WIDTH = 128
CAP = 80
MESH = pl.DeviceIdType.MESH
F32 = jnp.float32
BF16 = jnp.bfloat16
NT = (((1,), (1,)), ((), ()))


def remote(src, dst, send_sem, recv_sem, device):
    return pltpu.make_async_remote_copy(
        src_ref=src,
        dst_ref=dst,
        send_sem=send_sem,
        recv_sem=recv_sem,
        device_id=device,
        device_id_type=MESH,
    )


def greet(devices):
    barrier = pltpu.get_barrier_semaphore()
    for device in devices:
        pl.semaphore_signal(barrier, inc=1, device_id=device, device_id_type=MESH)
    pl.semaphore_wait(barrier, len(devices))


def block_kernel(
    n_y, n_z, n_t, order,
    q_hbm, k_ref, v_ref, w_ref, resid_ref, gain_hbm, router_hbm, ids_hbm, wg_ref, wu_ref, wd_ref,
    out_ref,
    q_ref, gain_ref, router_ref, ids_ref, mixed_ref, cols_ref, logit_ref,
    kv, w, scores, heads, a_part, a_peer, a_sums, a_cross, att, attn, res, sendn,
    wg, wu, wd, slots, xbuf, table, hidden, act_g, act_u, part, peer, cross, ybuf, zbuf, comb_hi,
    comb_lo, mix, fin,
    in_sem, res_sem,
    kv_ss, kv_rs, w_ss, w_rs, h_ss, h_rs, ap_ss, ap_rs, ax_ss, ax_rs, y_ss, y_rs,
    n_ss, n_rs, l_ss, l_rs,
    wsem, s_ss, s_rs, a_ss, a_rs, b_ss, b_rs, p_ss, p_rs, x_ss, x_rs, z_ss, z_rs, f_ss, f_rs,
):
    n_x = n_t // 2
    y, z, t = lax.axis_index("dp"), lax.axis_index("expert"), lax.axis_index("tensor")
    x, c = lax.div(t, 2), lax.rem(t, 2)
    right, left = lax.rem(z + 1, n_z), lax.rem(z + n_z - 1, n_z)
    rows = q_ref.shape[0]
    group = q_ref.shape[1] // HEAD_WIDTH
    width = mixed_ref.shape[1]
    ycols, tcols, trows, xcols = width // n_y, width // n_t, rows // n_t, width // n_x
    per = n_t // n_y
    half = w_ref.shape[0] // 2
    halves = 2
    per_half = n_z // halves
    n_groups = 4 if n_z % 4 == 0 else 2
    per_group = n_z // n_groups
    groups_half = n_groups // halves
    hrows, grows = per_half * CAP, per_group * CAP
    sibling_t = t + 1 - 2 * c
    sent = []

    def go(copy):
        copy.start()
        sent.append(copy)

    res_copy = pltpu.make_async_copy(
        resid_ref.at[pl.ds(pl.multiple_of(t * trows, trows), trows)], res, res_sem
    )
    first = [
        pltpu.make_async_copy(k_ref, kv.at[z, 0], in_sem.at[0]),
        pltpu.make_async_copy(v_ref, kv.at[z, 1], in_sem.at[1]),
        pltpu.make_async_copy(w_ref, w.at[z], in_sem.at[2]),
        pltpu.make_async_copy(q_hbm, q_ref, in_sem.at[3]),
    ]
    later = [
        pltpu.make_async_copy(gain_hbm, gain_ref, in_sem.at[4]),
        pltpu.make_async_copy(router_hbm, router_ref, in_sem.at[5]),
        pltpu.make_async_copy(ids_hbm, ids_ref, in_sem.at[6]),
        res_copy,
    ]
    for copy in first + later:
        copy.start()
    greet(
        [{"expert": lax.rem(z + d, n_z)} for d in range(1, n_z)]
        + [{"dp": lax.rem(y + d, n_y)} for d in range(1, n_y)]
        + [{"tensor": lax.rem(t + d, n_t)} for d in range(1, n_t)]
    )
    for copy in first:
        copy.wait()
    loads = []
    for i in range(n_x):
        span = pl.ds(i * xcols, xcols)
        loads.append(pltpu.make_async_copy(wg_ref.at[:, span], wg.at[i], wsem.at[0, i]))
        loads.append(pltpu.make_async_copy(wu_ref.at[:, span], wu.at[i], wsem.at[1, i]))
    for i in range(n_x):
        span = pl.ds(i * xcols, xcols)
        loads.append(pltpu.make_async_copy(wd_ref.at[:, span], wd.at[i], wsem.at[2, i]))
    for load in loads:
        load.start()

    hops = n_z // 2

    def kv_hop(way, s):
        block = lax.rem(z + (n_z - s if way == 0 else s), n_z)
        ref = kv.at[block, way] if s == hops - 1 else kv.at[block]
        return remote(
            ref, ref, kv_ss.at[way, s], kv_rs.at[way, s], {"expert": right if way == 0 else left}
        )

    def w_hop(way, s):
        block = lax.rem(z + (n_z - s if way == 0 else s), n_z)
        ref = w.at[block, pl.ds(way * half, half)] if s == hops - 1 else w.at[block]
        return remote(
            ref, ref, w_ss.at[way, s], w_rs.at[way, s], {"expert": right if way == 0 else left}
        )

    def score(block):
        for h in range(group):
            scores[block, h] = lax.dot_general(
                q_ref[:, h * HEAD_WIDTH : (h + 1) * HEAD_WIDTH],
                kv[block, 0],
                NT,
                preferred_element_type=F32,
            )

    for s in range(hops):
        for way in range(2):
            if s > 0:
                kv_hop(way, s - 1).wait_recv()
            go(kv_hop(way, s))
        for way in range(2):
            if s > 0:
                w_hop(way, s - 1).wait_recv()
            go(w_hop(way, s))
        score(lax.rem(z + n_z - s, n_z))
        if s > 0:
            score(lax.rem(z + s, n_z))
    for way in range(2):
        kv_hop(way, hops - 1).wait_recv()
    score(lax.rem(z + hops, n_z))

    all_values = kv[:, 1].reshape(n_z * rows, HEAD_WIDTH)
    shape = (rows, n_z * rows)
    causal = lax.broadcasted_iota(jnp.int32, shape, 1) <= (
        lax.broadcasted_iota(jnp.int32, shape, 0) + z * rows
    )
    for h in range(group):
        s_h = jnp.concatenate([scores[b, h] for b in range(n_z)], axis=1) * HEAD_WIDTH ** (-0.5)
        s_h = jnp.where(causal, s_h, -jnp.inf)
        e_h = jnp.exp(s_h - jnp.max(s_h, axis=1, keepdims=True))
        a_h = (e_h * (1.0 / jnp.sum(e_h, axis=1, keepdims=True))).astype(BF16)
        o_h = jnp.dot(a_h, all_values, preferred_element_type=F32)
        heads[y, :, h * HEAD_WIDTH : (h + 1) * HEAD_WIDTH] = o_h.astype(BF16)

    def heads_copy(d):
        return remote(
            heads.at[y], heads.at[y], h_ss.at[d - 1], h_rs.at[d - 1], {"dp": lax.rem(y + d, n_y)}
        )

    for d in range(1, n_y):
        go(heads_copy(d))
    for way in range(2):
        w_hop(way, hops - 1).wait_recv()

    sibling = {"tensor": t + 1 - 2 * c}
    w_all = w[...].reshape(ycols, w.shape[2])

    def head_pair(j):
        g = lax.rem(y + n_y - j, n_y)
        return remote(a_part.at[1 - c, g], a_peer.at[g], ap_ss.at[j], ap_rs.at[j], sibling)

    for j in range(n_y):
        g = lax.rem(y + n_y - j, n_y)
        if j > 0:
            heads_copy(j).wait_recv()
        pr = lax.dot_general(heads[g], w_all, NT, preferred_element_type=F32)
        pr = pr.astype(BF16).reshape(n_x, 2, trows, ycols)
        a_part[0, g] = pr[:, 0]
        a_part[1, g] = pr[:, 1]
        go(head_pair(j))
    for j in range(n_y):
        g = lax.rem(y + n_y - j, n_y)
        head_pair(j).wait_recv()
        a_sums[:, g] = (a_part[c, g].astype(F32) + a_peer[g].astype(F32)).astype(BF16)

    def head_cross(d):
        to = lax.rem(x + d, n_x)
        return remote(
            a_sums.at[to], a_cross.at[d - 1], ax_ss.at[d - 1], ax_rs.at[d - 1], {"tensor": to * 2 + c}
        )

    for d in range(1, n_x):
        go(head_cross(d))
    total = a_sums[x].astype(F32)
    for d in range(1, n_x):
        head_cross(d).wait_recv()
        total = total + a_cross[d - 1].astype(F32)
    att[...] = total.astype(BF16)

    def back_copy(d):
        to = lax.rem(y + d, n_y)
        return remote(att.at[to], attn.at[y], y_ss.at[d - 1], y_rs.at[d - 1], {"dp": to})

    for d in range(1, n_y):
        go(back_copy(d))
    attn[y] = att[y]
    for copy in later:
        copy.wait()
    for d in range(1, n_y):
        back_copy(d).wait_recv()

    mixed = []
    square = jnp.zeros((trows, 1), F32)
    for g in range(n_y):
        m_g = res[:, g * ycols : (g + 1) * ycols].astype(F32) + attn[g].astype(F32)
        mixed_ref[:, g * ycols : (g + 1) * ycols] = m_g
        square = square + jnp.sum(m_g * m_g, axis=1, keepdims=True)
        mixed.append(m_g)
    scale = lax.rsqrt(square * (1.0 / width) + 1e-05)
    logits = None
    for g in range(n_y):
        normed = (mixed[g] * scale * gain_ref[:, g * ycols : (g + 1) * ycols]).astype(BF16)
        for i in range(per):
            sendn[g * per + i] = normed[:, i * tcols : (i + 1) * tcols]
        term = lax.dot_general(
            normed,
            router_ref[:, g * ycols : (g + 1) * ycols],
            NT,
            preferred_element_type=F32,
        )
        logits = term if logits is None else logits + term
    lane = lax.broadcasted_iota(jnp.int32, (trows, 128), 1)
    wide = jnp.zeros((trows, 128), F32)
    for e in range(router_ref.shape[0]):
        wide = jnp.where(lane == e, logits[:, e : e + 1], wide)
    logit_ref[t] = wide
    cols_ref[t] = sendn[t]

    def cols_copy(d):
        to = lax.rem(t + d, n_t)
        return remote(
            sendn.at[to], cols_ref.at[t], n_ss.at[d - 1], n_rs.at[d - 1], {"tensor": to}
        )

    def logit_copy(d):
        to = lax.rem(t + d, n_t)
        return remote(
            logit_ref.at[t], logit_ref.at[t], l_ss.at[d - 1], l_rs.at[d - 1], {"tensor": to}
        )

    for d in range(1, n_t):
        go(cols_copy(d))
        go(logit_copy(d))
    for d in range(1, n_t):
        cols_copy(d).wait_recv()
        logit_copy(d).wait_recv()

    ids = ids_ref[...]
    n_e = table.shape[0]
    expert = lax.broadcasted_iota(jnp.int32, (n_e, rows), 0)
    named = ids[0:1, :] == expert
    for j in range(1, ids.shape[0]):
        named = jnp.logical_or(named, ids[j : j + 1, :] == expert)
    earlier = (
        lax.broadcasted_iota(jnp.int32, (rows, rows), 0)
        < lax.broadcasted_iota(jnp.int32, (rows, rows), 1)
    )
    before = jnp.dot(
        jnp.where(named, 1.0, 0.0).astype(BF16),
        jnp.where(earlier, 1.0, 0.0).astype(BF16),
        preferred_element_type=F32,
    )
    table[...] = jnp.where(named, before.astype(jnp.int32), -1)
    slot = lax.broadcasted_iota(jnp.int32, (CAP, rows), 0)
    cols = cols_ref[...].reshape(rows, tcols)

    def slot_copy(p):
        to = lax.rem(z + n_z - order[p], n_z)
        return remote(
            slots.at[p],
            xbuf.at[t, pl.ds(p * CAP, CAP)],
            s_ss.at[p],
            s_rs.at[p],
            {"expert": to},
        )

    for p in range(n_z):
        e = lax.rem(z + n_z - order[p], n_z)
        pick = jnp.where(table[pl.ds(e, 1), :] == slot, 1.0, 0.0).astype(BF16)
        picked = jnp.dot(pick, cols, preferred_element_type=F32).astype(BF16)
        if p == 0:
            xbuf[t, 0:CAP] = picked
        else:
            slots[p] = picked
            go(slot_copy(p))

    def share_copy(g, d):
        ref = xbuf.at[t, pl.ds(g * grows, grows)]
        to = lax.rem(x + d, n_x) * 2 + c
        return remote(ref, ref, a_ss.at[g, d - 1], a_rs.at[g, d - 1], {"tensor": to})

    def pass_copy(g, d):
        held = lax.rem(x + n_x - d, n_x) * 2 + c
        ref = xbuf.at[held, pl.ds(g * grows, grows)]
        return remote(ref, ref, b_ss.at[g, d], b_rs.at[g, d], {"tensor": sibling_t})

    def share(g):
        for p in range(g * per_group, (g + 1) * per_group):
            if p > 0:
                slot_copy(p).wait_recv()
        for d in range(1, n_x):
            go(share_copy(g, d))
        go(pass_copy(g, 0))

    def forward(g, d):
        share_copy(g, d).wait_recv()
        go(pass_copy(g, d))

    def arrive(g, d):
        pass_copy(g, d).wait_recv()

    def gate_up(h, d):
        i = lax.rem(x + n_x - d, n_x)
        span = pl.ds(h * hrows, hrows)
        held = jnp.concatenate([xbuf[i * 2, span], xbuf[i * 2 + 1, span]], axis=1)
        g_term = lax.dot_general(held, wg[i], NT, preferred_element_type=F32)
        act_g[...] = g_term if d == 0 else act_g[...] + g_term
        u_term = lax.dot_general(held, wu[i], NT, preferred_element_type=F32)
        act_u[...] = u_term if d == 0 else act_u[...] + u_term

    def pair_copy(h, d):
        i = lax.rem(x + d, n_x)
        return remote(
            part.at[h, 1 - c, i], peer.at[h, i], p_ss.at[h, d], p_rs.at[h, d],
            {"tensor": sibling_t},
        )

    def down(h):
        g_all = act_g[...]
        hidden[...] = (g_all / (1.0 + jnp.exp(-g_all)) * act_u[...]).astype(BF16)
        for d in list(range(1, n_x)) + [0]:
            i = lax.rem(x + d, n_x)
            o = jnp.dot(hidden[...], wd[i], preferred_element_type=F32).astype(BF16)
            part[h, 0, i] = o[:, :tcols]
            part[h, 1, i] = o[:, tcols:]
            go(pair_copy(h, d))

    def cross_copy(h, d):
        to = lax.rem(x + d, n_x)
        return remote(
            part.at[h, c, to], cross.at[h, d - 1], x_ss.at[h, d - 1], x_rs.at[h, d - 1],
            {"tensor": to * 2 + c},
        )

    def reduce_send(h):
        for d in list(range(1, n_x)) + [0]:
            i = lax.rem(x + d, n_x)
            pair_copy(h, d).wait_recv()
            part[h, c, i] = (part[h, c, i].astype(F32) + peer[h, i].astype(F32)).astype(BF16)
            if d > 0:
                go(cross_copy(h, d))

    def return_copy(p):
        to = lax.rem(z + order[p], n_z)
        return remote(
            ybuf.at[p], zbuf.at[pl.ds(p * CAP, CAP)], z_ss.at[p], z_rs.at[p], {"expert": to}
        )

    def reduce_recv(h):
        total = part[h, c, x].astype(F32)
        for d in range(1, n_x):
            cross_copy(h, d).wait_recv()
            total = total + cross[h, d - 1].astype(F32)
        total = total.astype(BF16)
        for i in range(per_half):
            p = h * per_half + i
            block = total[i * CAP : (i + 1) * CAP]
            if p == 0:
                zbuf[0:CAP] = block
            else:
                ybuf[p] = block
                go(return_copy(p))

    def of_half(h):
        return range(h * groups_half, (h + 1) * groups_half)

    for g in range(n_groups):
        share(g)
    gates = jnp.transpose(logit_ref[...].reshape(rows, 128))[0:n_e]
    gates = 1.0 / (1.0 + jnp.exp(-gates))
    pieces = []
    for p in range(n_z):
        e = lax.rem(z + n_z - order[p], n_z)
        pick = jnp.where(expert == e, gates, 0.0)
        pick = jnp.sum(pick, axis=0, keepdims=True)
        pieces.append(jnp.where(table[pl.ds(e, 1), :] == slot, pick, 0.0))
    comb = jnp.transpose(jnp.concatenate(pieces, axis=0))
    high = comb.astype(BF16)
    comb_hi[...] = high
    comb_lo[...] = (comb - high.astype(F32)).astype(BF16)
    for load in loads:
        load.wait()
    for h in range(halves):
        for d in list(range(0, n_x)):
            for g in of_half(h):
                if d > 0:
                    forward(g, d)
            for g in of_half(h):
                arrive(g, d)
            gate_up(h, d)
        down(h)
        reduce_send(h)
    for h in range(halves):
        reduce_recv(h)
    for p in range(1, n_z):
        return_copy(p).wait_recv()

    back = zbuf[...]
    mixture = jnp.dot(comb_hi[...], back, preferred_element_type=F32) + jnp.dot(
        comb_lo[...], back, preferred_element_type=F32
    )
    mix[...] = mixture.astype(BF16).reshape(n_t, trows, tcols)

    def final_copy(d):
        to = lax.rem(t + d, n_t)
        return remote(mix.at[to], fin.at[t], f_ss.at[d - 1], f_rs.at[d - 1], {"tensor": to})

    for d in range(1, n_t):
        go(final_copy(d))
    fin[t] = mix[t]
    for d in range(1, n_t):
        final_copy(d).wait_recv()
    for i in range(n_t):
        span = slice(i * tcols, (i + 1) * tcols)
        out_ref[:, span] = (mixed_ref[:, span] + fin[i].astype(F32)).astype(BF16)

    for copy in sent:
        copy.wait_send()


def slot_order(n_z):
    if n_z == 8:
        return (0, 1, 7, 2, 6, 3, 5, 4)
    return tuple(range(n_z))


def local(
    resid, queries, keys, values, out_weight, norm_gain, router_weight,
    gate_weight, up_weight, down_weight, expert_ids,
):
    n_y, n_z, n_t = lax.axis_size("dp"), lax.axis_size("expert"), lax.axis_size("tensor")
    n_x = n_t // 2
    rows, qcols = queries.shape[1], queries.shape[2]
    width = resid.shape[2]
    ff = gate_weight.shape[2]
    n_e = router_weight.shape[1]
    top = expert_ids.shape[2]
    ycols, tcols, trows, xcols = width // n_y, width // n_t, rows // n_t, width // n_x
    wcols = out_weight.shape[1]
    hrows = n_z // 2 * CAP
    hbm = pl.BlockSpec(memory_space=pltpu.HBM)
    dma = pltpu.SemaphoreType.DMA
    V = pltpu.VMEM
    hops = n_z // 2

    out = pl.pallas_call(
        functools.partial(block_kernel, n_y, n_z, n_t, slot_order(n_z)),
        out_shape=jax.ShapeDtypeStruct((trows, width), BF16),
        in_specs=[hbm] * 11,
        out_specs=pl.BlockSpec(memory_space=pltpu.VMEM),
        scratch_shapes=[
            V((rows, qcols), BF16),
            V((1, width), F32),
            V((n_e, width), BF16),
            V((top, rows), jnp.int32),
            V((trows, width), F32),
            V((n_t, trows, tcols), BF16),
            V((n_t, trows, 128), F32),
            V((n_z, 2, rows, HEAD_WIDTH), BF16),
            V((n_z, wcols, qcols), BF16),
            V((n_z, qcols // HEAD_WIDTH, rows, rows), F32),
            V((n_y, rows, qcols), BF16),
            V((2, n_y, n_x, trows, ycols), BF16),
            V((n_y, n_x, trows, ycols), BF16),
            V((n_x, n_y, trows, ycols), BF16),
            V((n_x - 1, n_y, trows, ycols), BF16),
            V((n_y, trows, ycols), BF16),
            V((n_y, trows, ycols), BF16),
            V((trows, width), BF16),
            V((n_t, trows, tcols), BF16),
            V((n_x, ff, xcols), BF16),
            V((n_x, ff, xcols), BF16),
            V((n_x, ff, xcols), BF16),
            V((n_z, CAP, tcols), BF16),
            V((n_t, n_z * CAP, tcols), BF16),
            V((n_e, rows), jnp.int32),
            V((hrows, ff), BF16),
            V((hrows, ff), F32),
            V((hrows, ff), F32),
            V((2, 2, n_x, hrows, tcols), BF16),
            V((2, n_x, hrows, tcols), BF16),
            V((2, n_x - 1, hrows, tcols), BF16),
            V((n_z, CAP, tcols), BF16),
            V((n_z * CAP, tcols), BF16),
            V((rows, n_z * CAP), BF16),
            V((rows, n_z * CAP), BF16),
            V((n_t, trows, tcols), BF16),
            V((n_t, trows, tcols), BF16),
            dma((7,)), dma,
            dma((2, hops)), dma((2, hops)), dma((2, hops)), dma((2, hops)),
            dma((n_y - 1,)), dma((n_y - 1,)), dma((n_y,)), dma((n_y,)),
            dma((n_x - 1,)), dma((n_x - 1,)), dma((n_y - 1,)), dma((n_y - 1,)),
            dma((n_t - 1,)), dma((n_t - 1,)), dma((n_t - 1,)), dma((n_t - 1,)),
            dma((3, n_x)),
            dma((n_z,)), dma((n_z,)),
            dma((4, n_x - 1)), dma((4, n_x - 1)), dma((4, n_x)), dma((4, n_x)),
            dma((2, n_x)), dma((2, n_x)), dma((2, n_x - 1)), dma((2, n_x - 1)),
            dma((n_z,)), dma((n_z,)), dma((n_t - 1,)), dma((n_t - 1,)),
        ],
        compiler_params=pltpu.CompilerParams(
            collective_id=0, has_side_effects=True, vmem_limit_bytes=58 * 2**20
        ),
    )(
        queries[0], keys[0], values[0], out_weight.T, resid[0], norm_gain[None],
        router_weight.T, expert_ids[0].T,
        jnp.swapaxes(gate_weight, 1, 2)[0], jnp.swapaxes(up_weight, 1, 2)[0], down_weight[0],
    )
    return out[None]


def solution(mesh):
    return jax.shard_map(
        local,
        mesh=mesh,
        in_specs=(
            P("dp", "expert", None),
            P("dp", "expert", "tensor"),
            P("dp", "expert", "tensor"),
            P("dp", "expert", "tensor"),
            P("tensor", ("dp", "expert")),
            P(),
            P(),
            P("expert", None, "tensor"),
            P("expert", None, "tensor"),
            P("expert", "tensor", None),
            P("dp", "expert", None),
        ),
        out_specs=P("dp", ("expert", "tensor"), None),
        check_vma=False,
    )
```

```python
import functools

import jax
import jax.numpy as jnp
from jax import lax
from jax.experimental import pallas as pl
from jax.experimental.pallas import tpu as pltpu
from jax.sharding import PartitionSpec as P

HEAD_WIDTH = 128
CAP = 80
MESH = pl.DeviceIdType.MESH
F32 = jnp.float32
BF16 = jnp.bfloat16
NT = (((1,), (1,)), ((), ()))


def remote(src, dst, send_sem, recv_sem, device):
    return pltpu.make_async_remote_copy(
        src_ref=src,
        dst_ref=dst,
        send_sem=send_sem,
        recv_sem=recv_sem,
        device_id=device,
        device_id_type=MESH,
    )


def greet(devices):
    barrier = pltpu.get_barrier_semaphore()
    for device in devices:
        pl.semaphore_signal(barrier, inc=1, device_id=device, device_id_type=MESH)
    pl.semaphore_wait(barrier, len(devices))


def block_kernel(
    n_y, n_z, n_t, order,
    q_hbm, k_ref, v_ref, w_ref, resid_ref, gain_hbm, router_hbm, ids_hbm, wg_ref, wu_ref, wd_ref,
    out_ref,
    q_ref, gain_ref, router_ref, ids_all, mixed_ref, zc, logit_ref,
    kv, w, scores, heads, a_part, a_peer, a_sums, a_cross, att, attn, res, sendn,
    wg, wu, wd, xbuf, table, mine, hidden, act_g, act_u, part, peer, vbuf, cross, ybuf, zbuf,
    comb_hi, comb_lo, mix, fin,
    in_sem, res_sem,
    kv_ss, kv_rs, w_ss, w_rs, h_ss, h_rs, ap_ss, ap_rs, ax_ss, ax_rs, y_ss, y_rs,
    n_ss, n_rs, l_ss, l_rs, i_ss, i_rs,
    wsem, s_ss, s_rs, a_ss, a_rs, b_ss, b_rs, p_ss, p_rs, v_ss, v_rs, x_ss, x_rs, z_ss, z_rs,
    f_ss, f_rs,
):
    n_x = n_t // 2
    y, z, t = lax.axis_index("dp"), lax.axis_index("expert"), lax.axis_index("tensor")
    x, c = lax.div(t, 2), lax.rem(t, 2)
    right, left = lax.rem(z + 1, n_z), lax.rem(z + n_z - 1, n_z)
    rows = q_ref.shape[0]
    group = q_ref.shape[1] // HEAD_WIDTH
    width = mixed_ref.shape[1]
    ycols, tcols, trows, xcols = width // n_y, width // n_t, rows // n_t, width // n_x
    per = n_t // n_y
    half = w_ref.shape[0] // 2
    halves = 2
    per_half = n_z // halves
    n_units = 4 if n_z % 4 == 0 else 2
    per_unit = n_z // n_units
    units_half = n_units // halves
    hrows, urows = per_half * CAP, per_unit * CAP
    near = (1, n_x - 1) if n_x > 2 else (1,)
    sibling_t = t + 1 - 2 * c
    sent = []

    def go(copy):
        copy.start()
        sent.append(copy)

    res_copy = pltpu.make_async_copy(
        resid_ref.at[pl.ds(pl.multiple_of(t * trows, trows), trows)], res, res_sem
    )
    first = [
        pltpu.make_async_copy(k_ref, kv.at[z, 0], in_sem.at[0]),
        pltpu.make_async_copy(v_ref, kv.at[z, 1], in_sem.at[1]),
        pltpu.make_async_copy(w_ref, w.at[z], in_sem.at[2]),
        pltpu.make_async_copy(q_hbm, q_ref, in_sem.at[3]),
        pltpu.make_async_copy(ids_hbm, ids_all.at[z], in_sem.at[6]),
    ]
    later = [
        pltpu.make_async_copy(gain_hbm, gain_ref, in_sem.at[4]),
        pltpu.make_async_copy(router_hbm, router_ref, in_sem.at[5]),
        res_copy,
    ]
    for copy in first + later:
        copy.start()
    greet(
        [{"expert": lax.rem(z + d, n_z)} for d in range(1, n_z)]
        + [{"dp": lax.rem(y + d, n_y)} for d in range(1, n_y)]
        + [{"tensor": lax.rem(t + d, n_t)} for d in range(1, n_t)]
    )
    for copy in first:
        copy.wait()
    loads = []
    for i in range(n_x):
        span = pl.ds(i * xcols, xcols)
        loads.append(pltpu.make_async_copy(wg_ref.at[:, span], wg.at[i], wsem.at[0, i]))
        loads.append(pltpu.make_async_copy(wu_ref.at[:, span], wu.at[i], wsem.at[1, i]))
    for i in range(n_x):
        span = pl.ds(i * xcols, xcols)
        loads.append(pltpu.make_async_copy(wd_ref.at[:, span], wd.at[i], wsem.at[2, i]))
    for load in loads:
        load.start()

    hops = n_z // 2

    def kv_hop(way, s):
        block = lax.rem(z + (n_z - s if way == 0 else s), n_z)
        ref = kv.at[block, way] if s == hops - 1 else kv.at[block]
        return remote(
            ref, ref, kv_ss.at[way, s], kv_rs.at[way, s], {"expert": right if way == 0 else left}
        )

    def w_hop(way, s):
        block = lax.rem(z + (n_z - s if way == 0 else s), n_z)
        ref = w.at[block, pl.ds(way * half, half)] if s == hops - 1 else w.at[block]
        return remote(
            ref, ref, w_ss.at[way, s], w_rs.at[way, s], {"expert": right if way == 0 else left}
        )

    def score(block):
        for h in range(group):
            scores[block, h] = lax.dot_general(
                q_ref[:, h * HEAD_WIDTH : (h + 1) * HEAD_WIDTH],
                kv[block, 0],
                NT,
                preferred_element_type=F32,
            )

    def w_step(s):
        for way in range(2):
            if s > 0:
                w_hop(way, s - 1).wait_recv()
            if s < hops:
                go(w_hop(way, s))

    def ids_copy(d):
        to = lax.rem(z + d, n_z)
        return remote(
            ids_all.at[z], ids_all.at[z], i_ss.at[d - 1], i_rs.at[d - 1], {"expert": to}
        )

    w_done = 0
    for s in range(hops):
        for way in range(2):
            if s > 0:
                kv_hop(way, s - 1).wait_recv()
            go(kv_hop(way, s))
        if s % 2 == 1:
            w_step(w_done)
            w_done += 1
        score(lax.rem(z + n_z - s, n_z))
        if s > 0:
            score(lax.rem(z + s, n_z))
    for way in range(2):
        kv_hop(way, hops - 1).wait_recv()
    score(lax.rem(z + hops, n_z))
    for d in range(1, n_z):
        go(ids_copy(d))

    def heads_copy(d, h):
        return remote(
            heads.at[y, h], heads.at[y, h], h_ss.at[d - 1, h], h_rs.at[d - 1, h],
            {"dp": lax.rem(y + d, n_y)},
        )

    all_values = kv[:, 1].reshape(n_z * rows, HEAD_WIDTH)
    shape = (rows, n_z * rows)
    causal = lax.broadcasted_iota(jnp.int32, shape, 1) <= (
        lax.broadcasted_iota(jnp.int32, shape, 0) + z * rows
    )
    for h in range(group):
        s_h = jnp.concatenate([scores[b, h] for b in range(n_z)], axis=1) * HEAD_WIDTH ** (-0.5)
        s_h = jnp.where(causal, s_h, -jnp.inf)
        e_h = jnp.exp(s_h - jnp.max(s_h, axis=1, keepdims=True))
        a_h = (e_h * (1.0 / jnp.sum(e_h, axis=1, keepdims=True))).astype(BF16)
        o_h = jnp.dot(a_h, all_values, preferred_element_type=F32)
        heads[y, h] = o_h.astype(BF16)
        for d in range(1, n_y):
            go(heads_copy(d, h))
        if h % 2 == 0 and w_done < hops:
            w_step(w_done)
            w_done += 1
    while w_done <= hops:
        w_step(w_done)
        w_done += 1

    sibling = {"tensor": t + 1 - 2 * c}
    w_all = w[...].reshape(ycols, w.shape[2])

    def head_pair(j):
        g = lax.rem(y + n_y - j, n_y)
        return remote(a_part.at[1 - c, g], a_peer.at[g], ap_ss.at[j], ap_rs.at[j], sibling)

    for j in range(n_y):
        g = lax.rem(y + n_y - j, n_y)
        if j > 0:
            for h in range(group):
                heads_copy(j, h).wait_recv()
        held = jnp.concatenate([heads[g, h] for h in range(group)], axis=1)
        pr = lax.dot_general(held, w_all, NT, preferred_element_type=F32)
        pr = pr.astype(BF16).reshape(n_x, 2, trows, ycols)
        a_part[0, g] = pr[:, 0]
        a_part[1, g] = pr[:, 1]
        go(head_pair(j))
    for j in range(n_y):
        g = lax.rem(y + n_y - j, n_y)
        head_pair(j).wait_recv()
        a_sums[:, g] = (a_part[c, g].astype(F32) + a_peer[g].astype(F32)).astype(BF16)

    def head_cross(d):
        to = lax.rem(x + d, n_x)
        return remote(
            a_sums.at[to], a_cross.at[d - 1], ax_ss.at[d - 1], ax_rs.at[d - 1], {"tensor": to * 2 + c}
        )

    for d in range(1, n_x):
        go(head_cross(d))
    total = a_sums[x].astype(F32)
    for d in range(1, n_x):
        head_cross(d).wait_recv()
        total = total + a_cross[d - 1].astype(F32)
    att[...] = total.astype(BF16)

    def back_copy(d):
        to = lax.rem(y + d, n_y)
        return remote(att.at[to], attn.at[y], y_ss.at[d - 1], y_rs.at[d - 1], {"dp": to})

    for d in range(1, n_y):
        go(back_copy(d))
    attn[y] = att[y]
    for copy in later:
        copy.wait()
    for d in range(1, n_y):
        back_copy(d).wait_recv()

    mixed = []
    square = jnp.zeros((trows, 1), F32)
    for g in range(n_y):
        m_g = res[:, g * ycols : (g + 1) * ycols].astype(F32) + attn[g].astype(F32)
        mixed_ref[:, g * ycols : (g + 1) * ycols] = m_g
        square = square + jnp.sum(m_g * m_g, axis=1, keepdims=True)
        mixed.append(m_g)
    scale = lax.rsqrt(square * (1.0 / width) + 1e-05)
    def cols_copy(d):
        to = lax.rem(t + d, n_t)
        return remote(
            sendn.at[to], zc.at[z, t], n_ss.at[d - 1], n_rs.at[d - 1], {"tensor": to}
        )

    def logit_copy(d):
        to = lax.rem(t + d, n_t)
        return remote(
            logit_ref.at[t], logit_ref.at[t], l_ss.at[d - 1], l_rs.at[d - 1], {"tensor": to}
        )

    normed = []
    for g in range(n_y):
        n_g = (mixed[g] * scale * gain_ref[:, g * ycols : (g + 1) * ycols]).astype(BF16)
        for i in range(per):
            sendn[g * per + i] = n_g[:, i * tcols : (i + 1) * tcols]
        normed.append(n_g)
    for d in range(1, n_t):
        go(cols_copy(d))
    zc[z, t] = sendn[t]
    logits = None
    for g in range(n_y):
        term = lax.dot_general(
            normed[g],
            router_ref[:, g * ycols : (g + 1) * ycols],
            NT,
            preferred_element_type=F32,
        )
        logits = term if logits is None else logits + term
    lane = lax.broadcasted_iota(jnp.int32, (trows, 128), 1)
    wide = jnp.zeros((trows, 128), F32)
    for e in range(router_ref.shape[0]):
        wide = jnp.where(lane == e, logits[:, e : e + 1], wide)
    logit_ref[t] = wide
    for d in range(1, n_t):
        go(logit_copy(d))

    n_e = table.shape[0]
    expert = lax.broadcasted_iota(jnp.int32, (n_e, rows), 0)
    place = lax.broadcasted_iota(jnp.int32, (n_z, rows), 0)
    earlier = (
        lax.broadcasted_iota(jnp.int32, (rows, rows), 0)
        < lax.broadcasted_iota(jnp.int32, (rows, rows), 1)
    )
    earlier = jnp.where(earlier, 1.0, 0.0).astype(BF16)

    def slots_of(named):
        before = jnp.dot(
            jnp.where(named, 1.0, 0.0).astype(BF16), earlier, preferred_element_type=F32
        )
        return jnp.where(named, before.astype(jnp.int32), -1)

    for d in range(1, n_z):
        ids_copy(d).wait_recv()
    own = ids_all[z]
    named = own[0:1, :] == expert
    for j in range(1, own.shape[0]):
        named = jnp.logical_or(named, own[j : j + 1, :] == expert)
    table[...] = slots_of(named)
    named = jnp.zeros((n_z, rows), jnp.int32)
    for p in range(n_z):
        ids = ids_all[lax.rem(z + order[p], n_z)]
        hit = jnp.sum(jnp.where(ids == z, 1, 0), axis=0, keepdims=True)
        named = jnp.where(place == p, hit, named)
    mine[...] = slots_of(named > 0)
    for d in range(1, n_t):
        cols_copy(d).wait_recv()

    slot = lax.broadcasted_iota(jnp.int32, (CAP, rows), 0)

    def z_hop(way, s):
        block = lax.rem(z + (n_z - s if way == 0 else s), n_z)
        span = pl.ds(way * (n_t // 2), n_t // 2)
        ref = zc.at[block, span] if s == hops - 1 else zc.at[block]
        return remote(
            ref, ref, s_ss.at[way, s], s_rs.at[way, s], {"expert": right if way == 0 else left}
        )

    def chunk(held, p):
        return xbuf.at[held, pl.ds(p * CAP, CAP)]

    def share_copy(p, d):
        ref = chunk(t, p)
        to = lax.rem(x + d, n_x) * 2 + c
        return remote(ref, ref, a_ss.at[p, d - 1], a_rs.at[p, d - 1], {"tensor": to})

    def relay_copy(p):
        d = near[p % 2]
        ref = chunk(lax.rem(x + n_x - d, n_x) * 2 + c, p)
        to = lax.rem(x + d, n_x) * 2 + c
        return remote(ref, ref, a_ss.at[p, 1], a_rs.at[p, 1], {"tensor": to})

    def pass_copy(p, d):
        ref = chunk(lax.rem(x + n_x - d, n_x) * 2 + c, p)
        return remote(ref, ref, b_ss.at[p, d], b_rs.at[p, d], {"tensor": sibling_t})

    def share(p):
        block = zc[lax.rem(z + order[p], n_z)].reshape(rows, tcols)
        pick = jnp.where(mine[p : p + 1, :] == slot, 1.0, 0.0).astype(BF16)
        xbuf[t, p * CAP : (p + 1) * CAP] = jnp.dot(
            pick, block, preferred_element_type=F32
        ).astype(BF16)
        for d in near:
            go(share_copy(p, d))
        go(pass_copy(p, 0))

    done = set()

    def relay(p):
        if ("relay", p) in done:
            return
        done.add(("relay", p))
        for d in near if p % 2 == 0 else near[::-1]:
            share_copy(p, d).wait_recv()
            if n_x > 2 and d == near[p % 2]:
                go(relay_copy(p))
            go(pass_copy(p, d))

    def far(p):
        if n_x > 2 and ("far", p) not in done:
            relay(p)
            done.add(("far", p))
            relay_copy(p).wait_recv()
            go(pass_copy(p, 2))

    def gate_up(h, d):
        for p in range(h * per_half, (h + 1) * per_half):
            if d in near:
                relay(p)
            elif d > 0:
                far(p)
            pass_copy(p, d).wait_recv()
        i = lax.rem(x + n_x - d, n_x)
        span = pl.ds(h * hrows, hrows)
        held = jnp.concatenate([xbuf[i * 2, span], xbuf[i * 2 + 1, span]], axis=1)
        g_term = lax.dot_general(held, wg[i], NT, preferred_element_type=F32)
        act_g[h] = g_term if d == 0 else act_g[h] + g_term
        u_term = lax.dot_general(held, wu[i], NT, preferred_element_type=F32)
        act_u[h] = u_term if d == 0 else act_u[h] + u_term

    def pair_copy(h, d):
        i = lax.rem(x + d, n_x)
        return remote(
            part.at[h, 1 - c, i], peer.at[h, i], p_ss.at[h, d], p_rs.at[h, d],
            {"tensor": sibling_t},
        )

    targets = ([2] if n_x > 2 else []) + list(near) + [0]

    def down(h):
        g_all = act_g[h]
        hidden[...] = (g_all / (1.0 + jnp.exp(-g_all)) * act_u[h]).astype(BF16)
        for d in targets:
            i = lax.rem(x + d, n_x)
            o = jnp.dot(hidden[...], wd[i], preferred_element_type=F32).astype(BF16)
            part[h, 0, i] = o[:, :tcols]
            part[h, 1, i] = o[:, tcols:]
            go(pair_copy(h, d))

    def pair_sum(h, d):
        i = lax.rem(x + d, n_x)
        pair_copy(h, d).wait_recv()
        part[h, c, i] = (part[h, c, i].astype(F32) + peer[h, i].astype(F32)).astype(BF16)

    def unit(q, d):
        h = q // units_half
        span = pl.ds((q % units_half) * urows, urows)
        return part.at[h, c, lax.rem(x + d, n_x), span]

    def via_copy(q):
        to = lax.rem(x + near[q % 2], n_x) * 2 + c
        return remote(unit(q, 2), vbuf.at[q], v_ss.at[q], v_rs.at[q], {"tensor": to})

    def near_copy(q, d):
        k = near.index(d)
        to = lax.rem(x + d, n_x) * 2 + c
        return remote(unit(q, d), cross.at[q, k], x_ss.at[q, k], x_rs.at[q, k], {"tensor": to})

    def sum_first(q):
        if n_x > 2:
            go(via_copy(q))
            go(near_copy(q, near[1 - q % 2]))

    def sum_second(q):
        d = near[q % 2] if n_x > 2 else 1
        if n_x > 2:
            via_copy(q).wait_recv()
            ref = unit(q, d)
            ref[...] = (ref[...].astype(F32) + vbuf[q].astype(F32)).astype(BF16)
        go(near_copy(q, d))

    def return_copy(p):
        to = lax.rem(z + order[p], n_z)
        return remote(
            ybuf.at[p], zbuf.at[pl.ds(p * CAP, CAP)], z_ss.at[p], z_rs.at[p], {"expert": to}
        )

    def sum_last(q):
        total = unit(q, 0)[...].astype(F32)
        for k in range(len(near)):
            near_copy(q, near[k]).wait_recv()
            total = total + cross[q, k].astype(F32)
        total = total.astype(BF16)
        for i in list(range(per_unit))[::-1]:
            p = q * per_unit + i
            block = total[i * CAP : (i + 1) * CAP]
            if p == 0:
                zbuf[0:CAP] = block
            else:
                ybuf[p] = block
                go(return_copy(p))

    for way in range(2):
        go(z_hop(way, 0))
    share(0)
    fresh, older = [0], []
    for s in range(1, hops + 1):
        for way in range(2):
            z_hop(way, s - 1).wait_recv()
            if s < hops:
                go(z_hop(way, s))
        now = [2 * s - 1, 2 * s] if s < hops else [n_z - 1]
        for p in now:
            share(p)
        if s == 1:
            for load in loads:
                load.wait()
        if s == hops - 1:
            gate_up(0, 0)
        for p in fresh:
            relay(p)
        for p in older:
            far(p)
        fresh, older = now, fresh
    for d in near:
        gate_up(0, d)
    for p in range(n_z - 1):
        relay(p)
    if n_x > 2:
        gate_up(0, 2)
    relay(n_z - 1)
    if hops == 1:
        gate_up(0, 0)
    gate_up(1, 0)
    down(0)
    for d in near:
        gate_up(1, d)
    for d in targets:
        pair_sum(0, d)
    early = [q for q in range(1, units_half)]
    middle = list(range(units_half, n_units))
    for q in early:
        sum_first(q)
    for p in range(n_z):
        far(p)
    for q in early:
        sum_second(q)
    if n_x > 2:
        gate_up(1, 2)
    down(1)
    for d in targets:
        pair_sum(1, d)
    for q in middle:
        sum_first(q)
    for q in early:
        sum_last(q)
    for q in middle:
        sum_second(q)
    sum_first(0)
    for d in range(1, n_t):
        logit_copy(d).wait_recv()
    gates = jnp.transpose(logit_ref[...].reshape(rows, 128))[0:n_e]
    gates = 1.0 / (1.0 + jnp.exp(-gates))
    pieces = []
    for p in range(n_z):
        e = lax.rem(z + n_z - order[p], n_z)
        pick = jnp.where(expert == e, gates, 0.0)
        pick = jnp.sum(pick, axis=0, keepdims=True)
        pieces.append(jnp.where(table[pl.ds(e, 1), :] == slot, pick, 0.0))
    comb = jnp.transpose(jnp.concatenate(pieces, axis=0))
    high = comb.astype(BF16)
    comb_hi[...] = high
    comb_lo[...] = (comb - high.astype(F32)).astype(BF16)
    sum_second(0)
    for q in middle:
        sum_last(q)
    sum_last(0)
    for p in range(1, n_z):
        return_copy(p).wait_recv()

    back = zbuf[...]
    mixture = jnp.dot(comb_hi[...], back, preferred_element_type=F32) + jnp.dot(
        comb_lo[...], back, preferred_element_type=F32
    )
    mix[...] = mixture.astype(BF16).reshape(n_t, trows, tcols)

    def final_copy(d):
        to = lax.rem(t + d, n_t)
        return remote(mix.at[to], fin.at[t], f_ss.at[d - 1], f_rs.at[d - 1], {"tensor": to})

    for d in range(1, n_t):
        go(final_copy(d))
    fin[t] = mix[t]
    for d in range(1, n_t):
        final_copy(d).wait_recv()
    for i in range(n_t):
        span = slice(i * tcols, (i + 1) * tcols)
        out_ref[:, span] = (mixed_ref[:, span] + fin[i].astype(F32)).astype(BF16)

    for copy in sent:
        copy.wait_send()


def slot_order(n_z):
    if n_z == 8:
        return (0, 7, 1, 6, 2, 5, 3, 4)
    return tuple(range(n_z))


def local(
    resid, queries, keys, values, out_weight, norm_gain, router_weight,
    gate_weight, up_weight, down_weight, expert_ids,
):
    n_y, n_z, n_t = lax.axis_size("dp"), lax.axis_size("expert"), lax.axis_size("tensor")
    n_x = n_t // 2
    rows, qcols = queries.shape[1], queries.shape[2]
    width = resid.shape[2]
    ff = gate_weight.shape[2]
    n_e = router_weight.shape[1]
    top = expert_ids.shape[2]
    ycols, tcols, trows, xcols = width // n_y, width // n_t, rows // n_t, width // n_x
    wcols = out_weight.shape[1]
    group = qcols // HEAD_WIDTH
    ny1 = max(1, n_y - 1)
    n_units = 4 if n_z % 4 == 0 else 2
    len_near = 2 if n_x > 2 else 1
    hrows, urows = n_z // 2 * CAP, n_z // n_units * CAP
    hbm = pl.BlockSpec(memory_space=pltpu.HBM)
    dma = pltpu.SemaphoreType.DMA
    V = pltpu.VMEM
    hops = n_z // 2

    out = pl.pallas_call(
        functools.partial(block_kernel, n_y, n_z, n_t, slot_order(n_z)),
        out_shape=jax.ShapeDtypeStruct((trows, width), BF16),
        in_specs=[hbm] * 11,
        out_specs=pl.BlockSpec(memory_space=pltpu.VMEM),
        scratch_shapes=[
            V((rows, qcols), BF16),
            V((1, width), F32),
            V((n_e, width), BF16),
            V((n_z, top, rows), jnp.int32),
            V((trows, width), F32),
            V((n_z, n_t, trows, tcols), BF16),
            V((n_t, trows, 128), F32),
            V((n_z, 2, rows, HEAD_WIDTH), BF16),
            V((n_z, wcols, qcols), BF16),
            V((n_z, qcols // HEAD_WIDTH, rows, rows), F32),
            V((n_y, qcols // HEAD_WIDTH, rows, HEAD_WIDTH), BF16),
            V((2, n_y, n_x, trows, ycols), BF16),
            V((n_y, n_x, trows, ycols), BF16),
            V((n_x, n_y, trows, ycols), BF16),
            V((n_x - 1, n_y, trows, ycols), BF16),
            V((n_y, trows, ycols), BF16),
            V((n_y, trows, ycols), BF16),
            V((trows, width), BF16),
            V((n_t, trows, tcols), BF16),
            V((n_x, ff, xcols), BF16),
            V((n_x, ff, xcols), BF16),
            V((n_x, ff, xcols), BF16),
            V((n_t, n_z * CAP, tcols), BF16),
            V((n_e, rows), jnp.int32),
            V((n_z, rows), jnp.int32),
            V((hrows, ff), BF16),
            V((2, hrows, ff), F32),
            V((2, hrows, ff), F32),
            V((2, 2, n_x, hrows, tcols), BF16),
            V((2, n_x, hrows, tcols), BF16),
            V((n_units, urows, tcols), BF16),
            V((n_units, len_near, urows, tcols), BF16),
            V((n_z, CAP, tcols), BF16),
            V((n_z * CAP, tcols), BF16),
            V((rows, n_z * CAP), BF16),
            V((rows, n_z * CAP), BF16),
            V((n_t, trows, tcols), BF16),
            V((n_t, trows, tcols), BF16),
            dma((7,)), dma,
            dma((2, hops)), dma((2, hops)), dma((2, hops)), dma((2, hops)),
            dma((ny1, group)), dma((ny1, group)), dma((n_y,)), dma((n_y,)),
            dma((n_x - 1,)), dma((n_x - 1,)), dma((ny1,)), dma((ny1,)),
            dma((n_t - 1,)), dma((n_t - 1,)), dma((n_t - 1,)), dma((n_t - 1,)),
            dma((n_z - 1,)), dma((n_z - 1,)),
            dma((3, n_x)), dma((2, hops)), dma((2, hops)),
            dma((n_z, 3)), dma((n_z, 3)), dma((n_z, n_x)), dma((n_z, n_x)),
            dma((2, n_x)), dma((2, n_x)), dma((n_units,)), dma((n_units,)),
            dma((n_units, len_near)), dma((n_units, len_near)),
            dma((n_z,)), dma((n_z,)), dma((n_t - 1,)), dma((n_t - 1,)),
        ],
        compiler_params=pltpu.CompilerParams(
            collective_id=0, has_side_effects=True, vmem_limit_bytes=58 * 2**20
        ),
    )(
        queries[0], keys[0], values[0], out_weight.T, resid[0], norm_gain[None],
        router_weight.T, expert_ids[0].T,
        jnp.swapaxes(gate_weight, 1, 2)[0], jnp.swapaxes(up_weight, 1, 2)[0], down_weight[0],
    )
    return out[None]


def solution(mesh):
    return jax.shard_map(
        local,
        mesh=mesh,
        in_specs=(
            P("dp", "expert", None),
            P("dp", "expert", "tensor"),
            P("dp", "expert", "tensor"),
            P("dp", "expert", "tensor"),
            P("tensor", ("dp", "expert")),
            P(),
            P(),
            P("expert", None, "tensor"),
            P("expert", None, "tensor"),
            P("expert", "tensor", None),
            P("dp", "expert", None),
        ),
        out_specs=P("dp", ("expert", "tensor"), None),
        check_vma=False,
    )
```

```python
import functools

import jax
import jax.numpy as jnp
from jax import lax
from jax.experimental import pallas as pl
from jax.experimental.pallas import tpu as pltpu
from jax.sharding import PartitionSpec as P

HEAD_WIDTH = 128
CAP = 80
MESH = pl.DeviceIdType.MESH
F32 = jnp.float32
BF16 = jnp.bfloat16
NT = (((1,), (1,)), ((), ()))


def remote(src, dst, send_sem, recv_sem, device):
    return pltpu.make_async_remote_copy(
        src_ref=src,
        dst_ref=dst,
        send_sem=send_sem,
        recv_sem=recv_sem,
        device_id=device,
        device_id_type=MESH,
    )


def greet(devices):
    barrier = pltpu.get_barrier_semaphore()
    for device in devices:
        pl.semaphore_signal(barrier, inc=1, device_id=device, device_id_type=MESH)
    pl.semaphore_wait(barrier, len(devices))


def block_kernel(
    n_y, n_z, n_t, order,
    q_hbm, k_ref, v_ref, w_ref, resid_ref, gain_hbm, router_hbm, ids_hbm, wg_ref, wu_ref, wd_ref,
    out_ref,
    q_ref, gain_ref, router_ref, ids_ref, mixed_ref, cols_ref, logit_ref,
    kv, w, scores, heads, a_part, a_peer, a_sums, a_cross, att, attn, res, sendn,
    wg, wu, wd, slots, xbuf, table, hidden, act_g, act_u, part, peer, cross, ybuf, zbuf, comb_hi,
    comb_lo, mix, fin,
    in_sem, res_sem,
    kv_ss, kv_rs, w_ss, w_rs, h_ss, h_rs, ap_ss, ap_rs, ax_ss, ax_rs, y_ss, y_rs,
    n_ss, n_rs, l_ss, l_rs,
    wsem, s_ss, s_rs, a_ss, a_rs, b_ss, b_rs, p_ss, p_rs, x_ss, x_rs, z_ss, z_rs, f_ss, f_rs,
):
    n_x = n_t // 2
    y, z, t = lax.axis_index("dp"), lax.axis_index("expert"), lax.axis_index("tensor")
    x, c = lax.div(t, 2), lax.rem(t, 2)
    right, left = lax.rem(z + 1, n_z), lax.rem(z + n_z - 1, n_z)
    rows = q_ref.shape[0]
    group = q_ref.shape[1] // HEAD_WIDTH
    width = mixed_ref.shape[1]
    ycols, tcols, trows, xcols = width // n_y, width // n_t, rows // n_t, width // n_x
    per = n_t // n_y
    half = w_ref.shape[0] // 2
    halves = 2
    per_half = n_z // halves
    n_units = 4 if n_z % 4 == 0 else 2
    per_unit = n_z // n_units
    units_half = n_units // halves
    hrows, urows = per_half * CAP, per_unit * CAP
    near = (1, n_x - 1) if n_x > 2 else (1,)
    others = near + ((2,) if n_x > 2 else ())
    sibling_t = t + 1 - 2 * c
    sent = []

    def go(copy):
        copy.start()
        sent.append(copy)

    res_copy = pltpu.make_async_copy(
        resid_ref.at[pl.ds(pl.multiple_of(t * trows, trows), trows)], res, res_sem
    )
    first = [
        pltpu.make_async_copy(k_ref, kv.at[z, 0], in_sem.at[0]),
        pltpu.make_async_copy(v_ref, kv.at[z, 1], in_sem.at[1]),
        pltpu.make_async_copy(w_ref, w.at[z], in_sem.at[2]),
        pltpu.make_async_copy(q_hbm, q_ref, in_sem.at[3]),
    ]
    later = [
        pltpu.make_async_copy(gain_hbm, gain_ref, in_sem.at[4]),
        pltpu.make_async_copy(router_hbm, router_ref, in_sem.at[5]),
        pltpu.make_async_copy(ids_hbm, ids_ref, in_sem.at[6]),
        res_copy,
    ]
    for copy in first + later:
        copy.start()
    greet(
        [{"expert": lax.rem(z + d, n_z)} for d in range(1, n_z)]
        + [{"dp": lax.rem(y + d, n_y)} for d in range(1, n_y)]
        + [{"tensor": lax.rem(t + d, n_t)} for d in range(1, n_t)]
    )
    for copy in first:
        copy.wait()
    loads = []
    for i in range(n_x):
        span = pl.ds(i * xcols, xcols)
        loads.append(pltpu.make_async_copy(wg_ref.at[:, span], wg.at[i], wsem.at[0, i]))
        loads.append(pltpu.make_async_copy(wu_ref.at[:, span], wu.at[i], wsem.at[1, i]))
    for i in range(n_x):
        span = pl.ds(i * xcols, xcols)
        loads.append(pltpu.make_async_copy(wd_ref.at[:, span], wd.at[i], wsem.at[2, i]))
    for load in loads:
        load.start()

    hops = n_z // 2

    def kv_hop(way, s):
        block = lax.rem(z + (n_z - s if way == 0 else s), n_z)
        ref = kv.at[block, way] if s == hops - 1 else kv.at[block]
        return remote(
            ref, ref, kv_ss.at[way, s], kv_rs.at[way, s], {"expert": right if way == 0 else left}
        )

    def w_hop(way, s):
        block = lax.rem(z + (n_z - s if way == 0 else s), n_z)
        ref = w.at[block, pl.ds(way * half, half)] if s == hops - 1 else w.at[block]
        return remote(
            ref, ref, w_ss.at[way, s], w_rs.at[way, s], {"expert": right if way == 0 else left}
        )

    def score(block):
        for h in range(group):
            scores[block, h] = lax.dot_general(
                q_ref[:, h * HEAD_WIDTH : (h + 1) * HEAD_WIDTH],
                kv[block, 0],
                NT,
                preferred_element_type=F32,
            )

    for s in range(hops):
        for way in range(2):
            if s > 0:
                kv_hop(way, s - 1).wait_recv()
            go(kv_hop(way, s))
        for way in range(2):
            if s > 0:
                w_hop(way, s - 1).wait_recv()
            go(w_hop(way, s))
        score(lax.rem(z + n_z - s, n_z))
        if s > 0:
            score(lax.rem(z + s, n_z))
    for way in range(2):
        kv_hop(way, hops - 1).wait_recv()
    score(lax.rem(z + hops, n_z))

    def heads_copy(d, h):
        return remote(
            heads.at[y, h], heads.at[y, h], h_ss.at[d - 1, h], h_rs.at[d - 1, h],
            {"dp": lax.rem(y + d, n_y)},
        )

    all_values = kv[:, 1].reshape(n_z * rows, HEAD_WIDTH)
    shape = (rows, n_z * rows)
    causal = lax.broadcasted_iota(jnp.int32, shape, 1) <= (
        lax.broadcasted_iota(jnp.int32, shape, 0) + z * rows
    )
    for h in range(group):
        s_h = jnp.concatenate([scores[b, h] for b in range(n_z)], axis=1) * HEAD_WIDTH ** (-0.5)
        s_h = jnp.where(causal, s_h, -jnp.inf)
        e_h = jnp.exp(s_h - jnp.max(s_h, axis=1, keepdims=True))
        a_h = (e_h * (1.0 / jnp.sum(e_h, axis=1, keepdims=True))).astype(BF16)
        o_h = jnp.dot(a_h, all_values, preferred_element_type=F32)
        heads[y, h] = o_h.astype(BF16)
        for d in range(1, n_y):
            go(heads_copy(d, h))
    for way in range(2):
        w_hop(way, hops - 1).wait_recv()

    sibling = {"tensor": t + 1 - 2 * c}
    w_all = w[...].reshape(ycols, w.shape[2])

    def head_pair(j):
        g = lax.rem(y + n_y - j, n_y)
        return remote(a_part.at[1 - c, g], a_peer.at[g], ap_ss.at[j], ap_rs.at[j], sibling)

    for j in range(n_y):
        g = lax.rem(y + n_y - j, n_y)
        if j > 0:
            for h in range(group):
                heads_copy(j, h).wait_recv()
        held = jnp.concatenate([heads[g, h] for h in range(group)], axis=1)
        pr = lax.dot_general(held, w_all, NT, preferred_element_type=F32)
        pr = pr.astype(BF16).reshape(n_x, 2, trows, ycols)
        a_part[0, g] = pr[:, 0]
        a_part[1, g] = pr[:, 1]
        go(head_pair(j))
    for j in range(n_y):
        g = lax.rem(y + n_y - j, n_y)
        head_pair(j).wait_recv()
        a_sums[:, g] = (a_part[c, g].astype(F32) + a_peer[g].astype(F32)).astype(BF16)

    def head_cross(d):
        to = lax.rem(x + d, n_x)
        return remote(
            a_sums.at[to], a_cross.at[d - 1], ax_ss.at[d - 1], ax_rs.at[d - 1], {"tensor": to * 2 + c}
        )

    for d in range(1, n_x):
        go(head_cross(d))
    total = a_sums[x].astype(F32)
    for d in range(1, n_x):
        head_cross(d).wait_recv()
        total = total + a_cross[d - 1].astype(F32)
    att[...] = total.astype(BF16)

    def back_copy(d):
        to = lax.rem(y + d, n_y)
        return remote(att.at[to], attn.at[y], y_ss.at[d - 1], y_rs.at[d - 1], {"dp": to})

    for d in range(1, n_y):
        go(back_copy(d))
    attn[y] = att[y]
    for copy in later:
        copy.wait()
    for d in range(1, n_y):
        back_copy(d).wait_recv()

    mixed = []
    square = jnp.zeros((trows, 1), F32)
    for g in range(n_y):
        m_g = res[:, g * ycols : (g + 1) * ycols].astype(F32) + attn[g].astype(F32)
        mixed_ref[:, g * ycols : (g + 1) * ycols] = m_g
        square = square + jnp.sum(m_g * m_g, axis=1, keepdims=True)
        mixed.append(m_g)
    scale = lax.rsqrt(square * (1.0 / width) + 1e-05)
    def cols_copy(d):
        to = lax.rem(t + d, n_t)
        return remote(
            sendn.at[to], cols_ref.at[t], n_ss.at[d - 1], n_rs.at[d - 1], {"tensor": to}
        )

    def logit_copy(d):
        to = lax.rem(t + d, n_t)
        return remote(
            logit_ref.at[t], logit_ref.at[t], l_ss.at[d - 1], l_rs.at[d - 1], {"tensor": to}
        )

    normed = []
    for g in range(n_y):
        n_g = (mixed[g] * scale * gain_ref[:, g * ycols : (g + 1) * ycols]).astype(BF16)
        for i in range(per):
            sendn[g * per + i] = n_g[:, i * tcols : (i + 1) * tcols]
        normed.append(n_g)
    for d in range(1, n_t):
        go(cols_copy(d))
    cols_ref[t] = sendn[t]
    logits = None
    for g in range(n_y):
        term = lax.dot_general(
            normed[g],
            router_ref[:, g * ycols : (g + 1) * ycols],
            NT,
            preferred_element_type=F32,
        )
        logits = term if logits is None else logits + term
    lane = lax.broadcasted_iota(jnp.int32, (trows, 128), 1)
    wide = jnp.zeros((trows, 128), F32)
    for e in range(router_ref.shape[0]):
        wide = jnp.where(lane == e, logits[:, e : e + 1], wide)
    logit_ref[t] = wide
    for d in range(1, n_t):
        go(logit_copy(d))

    n_e = table.shape[0]
    expert = lax.broadcasted_iota(jnp.int32, (n_e, rows), 0)
    ids = ids_ref[...]
    named = ids[0:1, :] == expert
    for j in range(1, ids.shape[0]):
        named = jnp.logical_or(named, ids[j : j + 1, :] == expert)
    earlier = (
        lax.broadcasted_iota(jnp.int32, (rows, rows), 0)
        < lax.broadcasted_iota(jnp.int32, (rows, rows), 1)
    )
    before = jnp.dot(
        jnp.where(named, 1.0, 0.0).astype(BF16),
        jnp.where(earlier, 1.0, 0.0).astype(BF16),
        preferred_element_type=F32,
    )
    table[...] = jnp.where(named, before.astype(jnp.int32), -1)
    for d in range(1, n_t):
        cols_copy(d).wait_recv()

    slot = lax.broadcasted_iota(jnp.int32, (CAP, rows), 0)
    cols = cols_ref[...].reshape(rows, tcols)

    def chunk(held, p):
        return xbuf.at[held, pl.ds(p * CAP, CAP)]

    def slot_copy(p):
        to = lax.rem(z + n_z - order[p], n_z)
        return remote(slots.at[p], chunk(t, p), s_ss.at[p], s_rs.at[p], {"expert": to})

    def pick(p):
        e = lax.rem(z + n_z - order[p], n_z)
        hot = jnp.where(table[pl.ds(e, 1), :] == slot, 1.0, 0.0).astype(BF16)
        picked = jnp.dot(hot, cols, preferred_element_type=F32).astype(BF16)
        if p == 0:
            xbuf[t, 0:CAP] = picked
        else:
            slots[p] = picked
            go(slot_copy(p))

    def share_copy(p, d):
        ref = chunk(t, p)
        to = lax.rem(x + d, n_x) * 2 + c
        return remote(ref, ref, a_ss.at[p, d - 1], a_rs.at[p, d - 1], {"tensor": to})

    def pass_copy(p, d):
        ref = chunk(lax.rem(x + n_x - d, n_x) * 2 + c, p)
        return remote(ref, ref, b_ss.at[p, d], b_rs.at[p, d], {"tensor": sibling_t})

    def share(p):
        if p > 0:
            slot_copy(p).wait_recv()
        for d in others:
            go(share_copy(p, d))
        go(pass_copy(p, 0))

    def forward(p, d):
        share_copy(p, d).wait_recv()
        go(pass_copy(p, d))

    def of_half(h):
        return range(h * per_half, (h + 1) * per_half)

    def gate_up(h, d):
        for p in of_half(h):
            pass_copy(p, d).wait_recv()
        i = lax.rem(x + n_x - d, n_x)
        span = pl.ds(h * hrows, hrows)
        held = jnp.concatenate([xbuf[i * 2, span], xbuf[i * 2 + 1, span]], axis=1)
        g_term = lax.dot_general(held, wg[i], NT, preferred_element_type=F32)
        act_g[h] = g_term if d == 0 else act_g[h] + g_term
        u_term = lax.dot_general(held, wu[i], NT, preferred_element_type=F32)
        act_u[h] = u_term if d == 0 else act_u[h] + u_term

    def pair_copy(q, d):
        i = lax.rem(x + d, n_x)
        return remote(
            part.at[q, 1 - c, i], peer.at[q, i], p_ss.at[q, d], p_rs.at[q, d],
            {"tensor": sibling_t},
        )

    targets = others[::-1] + (0,)

    def activate(h):
        g_all = act_g[h]
        hidden[...] = (g_all / (1.0 + jnp.exp(-g_all)) * act_u[h]).astype(BF16)

    def down(first, last):
        base = first % units_half
        held = hidden[base * urows : (base + last - first) * urows]
        for d in targets:
            i = lax.rem(x + d, n_x)
            o = jnp.dot(held, wd[i], preferred_element_type=F32).astype(BF16)
            for q in range(first, last):
                o_q = o[(q - first) * urows : (q - first + 1) * urows]
                part[q, 0, i] = o_q[:, :tcols]
                part[q, 1, i] = o_q[:, tcols:]
                go(pair_copy(q, d))

    def cross_copy(q, d):
        to = lax.rem(x + d, n_x)
        return remote(
            part.at[q, c, to], cross.at[q, d - 1], x_ss.at[q, d - 1], x_rs.at[q, d - 1],
            {"tensor": to * 2 + c},
        )

    def reduce_send(q):
        for d in targets:
            i = lax.rem(x + d, n_x)
            pair_copy(q, d).wait_recv()
            part[q, c, i] = (part[q, c, i].astype(F32) + peer[q, i].astype(F32)).astype(BF16)
            if d > 0:
                go(cross_copy(q, d))

    def return_copy(p):
        to = lax.rem(z + order[p], n_z)
        return remote(
            ybuf.at[p], zbuf.at[pl.ds(p * CAP, CAP)], z_ss.at[p], z_rs.at[p], {"expert": to}
        )

    def reduce_recv(q):
        total = part[q, c, x].astype(F32)
        for d in near + others[len(near) :]:
            cross_copy(q, d).wait_recv()
            total = total + cross[q, d - 1].astype(F32)
        total = total.astype(BF16)
        for i in range(per_unit)[::-1]:
            p = q * per_unit + i
            block = total[i * CAP : (i + 1) * CAP]
            if p == 0:
                zbuf[0:CAP] = block
            else:
                ybuf[p] = block
                go(return_copy(p))

    for p in range(1, min(3, n_z)):
        pick(p)
    pick(0)
    share(0)
    for p in range(3, n_z):
        pick(p)
    for load in loads:
        load.wait()
    for p in range(1, n_z):
        share(p)
    gate_up(0, 0)
    for d in near:
        for p in of_half(0):
            forward(p, d)
    gate_up(1, 0)
    for d in near:
        gate_up(0, d)
    for d in others[len(near) :]:
        for p in of_half(0):
            forward(p, d)
        gate_up(0, d)
    activate(0)
    down(0, units_half)
    for d in near:
        for p in of_half(1):
            forward(p, d)
    for q in range(units_half)[::-1]:
        reduce_send(q)
    for d in near:
        gate_up(1, d)
    for d in others[len(near) :]:
        for p in of_half(1):
            forward(p, d)
        gate_up(1, d)
    activate(1)
    for q in range(units_half, n_units)[::-1]:
        down(q, q + 1)
        reduce_send(q)
    for q in range(units_half)[::-1]:
        reduce_recv(q)
    for d in range(1, n_t):
        logit_copy(d).wait_recv()
    gates = jnp.transpose(logit_ref[...].reshape(rows, 128))[0:n_e]
    gates = 1.0 / (1.0 + jnp.exp(-gates))
    pieces = []
    for p in range(n_z):
        e = lax.rem(z + n_z - order[p], n_z)
        gate = jnp.where(expert == e, gates, 0.0)
        gate = jnp.sum(gate, axis=0, keepdims=True)
        pieces.append(jnp.where(table[pl.ds(e, 1), :] == slot, gate, 0.0))
    comb = jnp.transpose(jnp.concatenate(pieces, axis=0))
    high = comb.astype(BF16)
    comb_hi[...] = high
    comb_lo[...] = (comb - high.astype(F32)).astype(BF16)
    for q in range(units_half, n_units)[::-1]:
        reduce_recv(q)
    for p in range(1, n_z):
        return_copy(p).wait_recv()

    back = zbuf[...]
    mixture = jnp.dot(comb_hi[...], back, preferred_element_type=F32) + jnp.dot(
        comb_lo[...], back, preferred_element_type=F32
    )
    mix[...] = mixture.astype(BF16).reshape(n_t, trows, tcols)

    def final_copy(d):
        to = lax.rem(t + d, n_t)
        return remote(mix.at[to], fin.at[t], f_ss.at[d - 1], f_rs.at[d - 1], {"tensor": to})

    for d in range(1, n_t):
        go(final_copy(d))
    fin[t] = mix[t]
    for d in range(1, n_t):
        final_copy(d).wait_recv()
    for i in range(n_t):
        span = slice(i * tcols, (i + 1) * tcols)
        out_ref[:, span] = (mixed_ref[:, span] + fin[i].astype(F32)).astype(BF16)

    for copy in sent:
        copy.wait_send()


def slot_order(n_z):
    if n_z == 8:
        return (0, 1, 7, 2, 6, 3, 5, 4)
    return tuple(range(n_z))


def local(
    resid, queries, keys, values, out_weight, norm_gain, router_weight,
    gate_weight, up_weight, down_weight, expert_ids,
):
    n_y, n_z, n_t = lax.axis_size("dp"), lax.axis_size("expert"), lax.axis_size("tensor")
    n_x = n_t // 2
    rows, qcols = queries.shape[1], queries.shape[2]
    width = resid.shape[2]
    ff = gate_weight.shape[2]
    n_e = router_weight.shape[1]
    top = expert_ids.shape[2]
    ycols, tcols, trows, xcols = width // n_y, width // n_t, rows // n_t, width // n_x
    wcols = out_weight.shape[1]
    group = qcols // HEAD_WIDTH
    n_units = 4 if n_z % 4 == 0 else 2
    hrows, urows = n_z // 2 * CAP, n_z // n_units * CAP
    hbm = pl.BlockSpec(memory_space=pltpu.HBM)
    dma = pltpu.SemaphoreType.DMA
    V = pltpu.VMEM
    hops = n_z // 2

    out = pl.pallas_call(
        functools.partial(block_kernel, n_y, n_z, n_t, slot_order(n_z)),
        out_shape=jax.ShapeDtypeStruct((trows, width), BF16),
        in_specs=[hbm] * 11,
        out_specs=pl.BlockSpec(memory_space=pltpu.VMEM),
        scratch_shapes=[
            V((rows, qcols), BF16),
            V((1, width), F32),
            V((n_e, width), BF16),
            V((top, rows), jnp.int32),
            V((trows, width), F32),
            V((n_t, trows, tcols), BF16),
            V((n_t, trows, 128), F32),
            V((n_z, 2, rows, HEAD_WIDTH), BF16),
            V((n_z, wcols, qcols), BF16),
            V((n_z, qcols // HEAD_WIDTH, rows, rows), F32),
            V((n_y, group, rows, HEAD_WIDTH), BF16),
            V((2, n_y, n_x, trows, ycols), BF16),
            V((n_y, n_x, trows, ycols), BF16),
            V((n_x, n_y, trows, ycols), BF16),
            V((n_x - 1, n_y, trows, ycols), BF16),
            V((n_y, trows, ycols), BF16),
            V((n_y, trows, ycols), BF16),
            V((trows, width), BF16),
            V((n_t, trows, tcols), BF16),
            V((n_x, ff, xcols), BF16),
            V((n_x, ff, xcols), BF16),
            V((n_x, ff, xcols), BF16),
            V((n_z, CAP, tcols), BF16),
            V((n_t, n_z * CAP, tcols), BF16),
            V((n_e, rows), jnp.int32),
            V((hrows, ff), BF16),
            V((2, hrows, ff), F32),
            V((2, hrows, ff), F32),
            V((n_units, 2, n_x, urows, tcols), BF16),
            V((n_units, n_x, urows, tcols), BF16),
            V((n_units, n_x - 1, urows, tcols), BF16),
            V((n_z, CAP, tcols), BF16),
            V((n_z * CAP, tcols), BF16),
            V((rows, n_z * CAP), BF16),
            V((rows, n_z * CAP), BF16),
            V((n_t, trows, tcols), BF16),
            V((n_t, trows, tcols), BF16),
            dma((7,)), dma,
            dma((2, hops)), dma((2, hops)), dma((2, hops)), dma((2, hops)),
            dma((n_y - 1, group)), dma((n_y - 1, group)), dma((n_y,)), dma((n_y,)),
            dma((n_x - 1,)), dma((n_x - 1,)), dma((n_y - 1,)), dma((n_y - 1,)),
            dma((n_t - 1,)), dma((n_t - 1,)), dma((n_t - 1,)), dma((n_t - 1,)),
            dma((3, n_x)),
            dma((n_z,)), dma((n_z,)),
            dma((n_z, n_x - 1)), dma((n_z, n_x - 1)), dma((n_z, n_x)), dma((n_z, n_x)),
            dma((n_units, n_x)), dma((n_units, n_x)),
            dma((n_units, n_x - 1)), dma((n_units, n_x - 1)),
            dma((n_z,)), dma((n_z,)), dma((n_t - 1,)), dma((n_t - 1,)),
        ],
        compiler_params=pltpu.CompilerParams(
            collective_id=0, has_side_effects=True, vmem_limit_bytes=58 * 2**20
        ),
    )(
        queries[0], keys[0], values[0], out_weight.T, resid[0], norm_gain[None],
        router_weight.T, expert_ids[0].T,
        jnp.swapaxes(gate_weight, 1, 2)[0], jnp.swapaxes(up_weight, 1, 2)[0], down_weight[0],
    )
    return out[None]


def solution(mesh):
    return jax.shard_map(
        local,
        mesh=mesh,
        in_specs=(
            P("dp", "expert", None),
            P("dp", "expert", "tensor"),
            P("dp", "expert", "tensor"),
            P("dp", "expert", "tensor"),
            P("tensor", ("dp", "expert")),
            P(),
            P(),
            P("expert", None, "tensor"),
            P("expert", None, "tensor"),
            P("expert", "tensor", None),
            P("dp", "expert", None),
        ),
        out_specs=P("dp", ("expert", "tensor"), None),
        check_vma=False,
    )
```

```python
import functools

import jax
import jax.numpy as jnp
from jax import lax
from jax.experimental import pallas as pl
from jax.experimental.pallas import tpu as pltpu
from jax.sharding import PartitionSpec as P

HEAD_WIDTH = 128
CAP = 80
MESH = pl.DeviceIdType.MESH
F32 = jnp.float32
BF16 = jnp.bfloat16
NT = (((1,), (1,)), ((), ()))


def remote(src, dst, send_sem, recv_sem, device):
    return pltpu.make_async_remote_copy(
        src_ref=src,
        dst_ref=dst,
        send_sem=send_sem,
        recv_sem=recv_sem,
        device_id=device,
        device_id_type=MESH,
    )


def greet(devices):
    barrier = pltpu.get_barrier_semaphore()
    for device in devices:
        pl.semaphore_signal(barrier, inc=1, device_id=device, device_id_type=MESH)
    pl.semaphore_wait(barrier, len(devices))


def block_kernel(
    n_y, n_z, n_t, order,
    q_hbm, k_ref, v_ref, w_ref, resid_ref, gain_hbm, router_hbm, ids_hbm, wg_ref, wu_ref, wd_ref,
    out_ref,
    q_ref, gain_ref, router_ref, ids_ref, mixed_ref, cols_ref, logit_ref,
    kv, w, scores, heads, a_part, a_peer, a_sums, a_cross, att, attn, res, sendn,
    wg, wu, wd, slots, xbuf, table, hidden, act_g, act_u, part, peer, cross, ybuf, zbuf, comb_hi,
    comb_lo, mix, fin,
    in_sem, res_sem,
    kv_ss, kv_rs, w_ss, w_rs, h_ss, h_rs, ap_ss, ap_rs, ax_ss, ax_rs, y_ss, y_rs,
    n_ss, n_rs, l_ss, l_rs,
    wsem, s_ss, s_rs, a_ss, a_rs, b_ss, b_rs, p_ss, p_rs, x_ss, x_rs, z_ss, z_rs, f_ss, f_rs,
):
    n_x = n_t // 2
    y, z, t = lax.axis_index("dp"), lax.axis_index("expert"), lax.axis_index("tensor")
    x, c = lax.div(t, 2), lax.rem(t, 2)
    right, left = lax.rem(z + 1, n_z), lax.rem(z + n_z - 1, n_z)
    rows = q_ref.shape[0]
    group = q_ref.shape[1] // HEAD_WIDTH
    width = mixed_ref.shape[1]
    ycols, tcols, trows, xcols = width // n_y, width // n_t, rows // n_t, width // n_x
    per = n_t // n_y
    half = w_ref.shape[0] // 2
    halves = 2
    per_half = n_z // halves
    n_units = 4 if n_z % 4 == 0 else 2
    per_unit = n_z // n_units
    units_half = n_units // halves
    hrows, urows = per_half * CAP, per_unit * CAP
    near = (1, n_x - 1) if n_x > 2 else (1,)
    others = near + ((2,) if n_x > 2 else ())
    sibling_t = t + 1 - 2 * c
    sent = []

    def go(copy):
        copy.start()
        sent.append(copy)

    res_copy = pltpu.make_async_copy(
        resid_ref.at[pl.ds(pl.multiple_of(t * trows, trows), trows)], res, res_sem
    )
    first = [
        pltpu.make_async_copy(k_ref, kv.at[z, 0], in_sem.at[0]),
        pltpu.make_async_copy(v_ref, kv.at[z, 1], in_sem.at[1]),
        pltpu.make_async_copy(w_ref, w.at[z], in_sem.at[2]),
        pltpu.make_async_copy(q_hbm, q_ref, in_sem.at[3]),
    ]
    later = [
        pltpu.make_async_copy(gain_hbm, gain_ref, in_sem.at[4]),
        pltpu.make_async_copy(router_hbm, router_ref, in_sem.at[5]),
        pltpu.make_async_copy(ids_hbm, ids_ref, in_sem.at[6]),
        res_copy,
    ]
    for copy in first + later:
        copy.start()
    greet(
        [{"expert": lax.rem(z + d, n_z)} for d in range(1, n_z)]
        + [{"dp": lax.rem(y + d, n_y)} for d in range(1, n_y)]
        + [{"tensor": lax.rem(t + d, n_t)} for d in range(1, n_t)]
    )
    for copy in first:
        copy.wait()
    loads = []
    for i in range(n_x):
        span = pl.ds(i * xcols, xcols)
        loads.append(pltpu.make_async_copy(wg_ref.at[:, span], wg.at[i], wsem.at[0, i]))
        loads.append(pltpu.make_async_copy(wu_ref.at[:, span], wu.at[i], wsem.at[1, i]))
    for i in range(n_x):
        span = pl.ds(i * xcols, xcols)
        loads.append(pltpu.make_async_copy(wd_ref.at[:, span], wd.at[i], wsem.at[2, i]))
    for load in loads:
        load.start()

    hops = n_z // 2

    def kv_hop(way, s):
        block = lax.rem(z + (n_z - s if way == 0 else s), n_z)
        ref = kv.at[block, way] if s == hops - 1 else kv.at[block]
        return remote(
            ref, ref, kv_ss.at[way, s], kv_rs.at[way, s], {"expert": right if way == 0 else left}
        )

    def w_hop(way, s):
        block = lax.rem(z + (n_z - s if way == 0 else s), n_z)
        ref = w.at[block, pl.ds(way * half, half)] if s == hops - 1 else w.at[block]
        return remote(
            ref, ref, w_ss.at[way, s], w_rs.at[way, s], {"expert": right if way == 0 else left}
        )

    def score(block):
        for h in range(group):
            scores[block, h] = lax.dot_general(
                q_ref[:, h * HEAD_WIDTH : (h + 1) * HEAD_WIDTH],
                kv[block, 0],
                NT,
                preferred_element_type=F32,
            )

    for s in range(hops):
        for way in range(2):
            if s > 0:
                kv_hop(way, s - 1).wait_recv()
            go(kv_hop(way, s))
        for way in range(2):
            if s > 0:
                w_hop(way, s - 1).wait_recv()
            go(w_hop(way, s))
        score(lax.rem(z + n_z - s, n_z))
        if s > 0:
            score(lax.rem(z + s, n_z))
    for way in range(2):
        kv_hop(way, hops - 1).wait_recv()
    score(lax.rem(z + hops, n_z))

    def heads_copy(d, h):
        return remote(
            heads.at[y, h], heads.at[y, h], h_ss.at[d - 1, h], h_rs.at[d - 1, h],
            {"dp": lax.rem(y + d, n_y)},
        )

    all_values = kv[:, 1].reshape(n_z * rows, HEAD_WIDTH)
    shape = (rows, n_z * rows)
    causal = lax.broadcasted_iota(jnp.int32, shape, 1) <= (
        lax.broadcasted_iota(jnp.int32, shape, 0) + z * rows
    )
    for h in range(group):
        s_h = jnp.concatenate([scores[b, h] for b in range(n_z)], axis=1) * HEAD_WIDTH ** (-0.5)
        s_h = jnp.where(causal, s_h, -jnp.inf)
        e_h = jnp.exp(s_h - jnp.max(s_h, axis=1, keepdims=True))
        a_h = (e_h * (1.0 / jnp.sum(e_h, axis=1, keepdims=True))).astype(BF16)
        o_h = jnp.dot(a_h, all_values, preferred_element_type=F32)
        heads[y, h] = o_h.astype(BF16)
        for d in range(1, n_y):
            go(heads_copy(d, h))
    for way in range(2):
        w_hop(way, hops - 1).wait_recv()

    sibling = {"tensor": t + 1 - 2 * c}
    w_all = w[...].reshape(ycols, w.shape[2])

    def head_pair(j):
        g = lax.rem(y + n_y - j, n_y)
        return remote(a_part.at[1 - c, g], a_peer.at[g], ap_ss.at[j], ap_rs.at[j], sibling)

    def head_cross(d, j):
        to = lax.rem(x + d, n_x)
        g = lax.rem(y + n_y - j, n_y)
        return remote(
            a_sums.at[to, g], a_cross.at[d - 1, g], ax_ss.at[d - 1, j], ax_rs.at[d - 1, j],
            {"tensor": to * 2 + c},
        )

    def head_sum(j):
        g = lax.rem(y + n_y - j, n_y)
        head_pair(j).wait_recv()
        a_sums[:, g] = (a_part[c, g].astype(F32) + a_peer[g].astype(F32)).astype(BF16)
        for d in others[::-1]:
            go(head_cross(d, j))

    turns = [0] + sorted(range(1, n_y), key=lambda d: min(d, n_y - d))
    for k, j in enumerate(turns):
        g = lax.rem(y + n_y - j, n_y)
        if j > 0:
            for h in range(group):
                heads_copy(j, h).wait_recv()
        held = jnp.concatenate([heads[g, h] for h in range(group)], axis=1)
        pr = lax.dot_general(held, w_all, NT, preferred_element_type=F32)
        pr = pr.astype(BF16).reshape(n_x, 2, trows, ycols)
        a_part[0, g] = pr[:, 0]
        a_part[1, g] = pr[:, 1]
        go(head_pair(j))
        if k > 0:
            head_sum(turns[k - 1])
    head_sum(turns[-1])

    def back_copy(d):
        to = lax.rem(y + d, n_y)
        return remote(att.at[to], attn.at[y], y_ss.at[d - 1], y_rs.at[d - 1], {"dp": to})

    for j in turns:
        g = lax.rem(y + n_y - j, n_y)
        total = a_sums[x, g].astype(F32)
        for d in others:
            head_cross(d, j).wait_recv()
            total = total + a_cross[d - 1, g].astype(F32)
        if j == 0:
            attn[y] = total.astype(BF16)
        else:
            att[g] = total.astype(BF16)
            go(back_copy(n_y - j))
    for copy in later:
        copy.wait()
    for d in range(1, n_y):
        back_copy(d).wait_recv()

    mixed = []
    square = jnp.zeros((trows, 1), F32)
    for g in range(n_y):
        m_g = res[:, g * ycols : (g + 1) * ycols].astype(F32) + attn[g].astype(F32)
        mixed_ref[:, g * ycols : (g + 1) * ycols] = m_g
        square = square + jnp.sum(m_g * m_g, axis=1, keepdims=True)
        mixed.append(m_g)
    scale = lax.rsqrt(square * (1.0 / width) + 1e-05)
    def cols_copy(d):
        to = lax.rem(t + d, n_t)
        return remote(
            sendn.at[to], cols_ref.at[t], n_ss.at[d - 1], n_rs.at[d - 1], {"tensor": to}
        )

    def logit_copy(d):
        to = lax.rem(t + d, n_t)
        return remote(
            logit_ref.at[t], logit_ref.at[t], l_ss.at[d - 1], l_rs.at[d - 1], {"tensor": to}
        )

    normed = []
    for g in range(n_y):
        n_g = (mixed[g] * scale * gain_ref[:, g * ycols : (g + 1) * ycols]).astype(BF16)
        for i in range(per):
            sendn[g * per + i] = n_g[:, i * tcols : (i + 1) * tcols]
        normed.append(n_g)
    for d in range(1, n_t):
        go(cols_copy(d))
    cols_ref[t] = sendn[t]
    logits = None
    for g in range(n_y):
        term = lax.dot_general(
            normed[g],
            router_ref[:, g * ycols : (g + 1) * ycols],
            NT,
            preferred_element_type=F32,
        )
        logits = term if logits is None else logits + term
    lane = lax.broadcasted_iota(jnp.int32, (trows, 128), 1)
    wide = jnp.zeros((trows, 128), F32)
    for e in range(router_ref.shape[0]):
        wide = jnp.where(lane == e, logits[:, e : e + 1], wide)
    logit_ref[t] = wide
    for d in range(1, n_t):
        go(logit_copy(d))

    n_e = table.shape[0]
    expert = lax.broadcasted_iota(jnp.int32, (n_e, rows), 0)
    ids = ids_ref[...]
    named = ids[0:1, :] == expert
    for j in range(1, ids.shape[0]):
        named = jnp.logical_or(named, ids[j : j + 1, :] == expert)
    earlier = (
        lax.broadcasted_iota(jnp.int32, (rows, rows), 0)
        < lax.broadcasted_iota(jnp.int32, (rows, rows), 1)
    )
    before = jnp.dot(
        jnp.where(named, 1.0, 0.0).astype(BF16),
        jnp.where(earlier, 1.0, 0.0).astype(BF16),
        preferred_element_type=F32,
    )
    table[...] = jnp.where(named, before.astype(jnp.int32), -1)
    for d in range(1, n_t):
        cols_copy(d).wait_recv()

    slot = lax.broadcasted_iota(jnp.int32, (CAP, rows), 0)
    cols = cols_ref[...].reshape(rows, tcols)

    def chunk(held, p):
        return xbuf.at[held, pl.ds(p * CAP, CAP)]

    def slot_copy(p):
        to = lax.rem(z + n_z - order[p], n_z)
        return remote(slots.at[p], chunk(t, p), s_ss.at[p], s_rs.at[p], {"expert": to})

    def pick(p):
        e = lax.rem(z + n_z - order[p], n_z)
        hot = jnp.where(table[pl.ds(e, 1), :] == slot, 1.0, 0.0).astype(BF16)
        picked = jnp.dot(hot, cols, preferred_element_type=F32).astype(BF16)
        if p == 0:
            xbuf[t, 0:CAP] = picked
        else:
            slots[p] = picked
            go(slot_copy(p))

    def share_copy(p, d):
        ref = chunk(t, p)
        to = lax.rem(x + d, n_x) * 2 + c
        return remote(ref, ref, a_ss.at[p, d - 1], a_rs.at[p, d - 1], {"tensor": to})

    def pass_copy(p, d):
        ref = chunk(lax.rem(x + n_x - d, n_x) * 2 + c, p)
        return remote(ref, ref, b_ss.at[p, d], b_rs.at[p, d], {"tensor": sibling_t})

    def share(p):
        if p > 0:
            slot_copy(p).wait_recv()
        for d in others:
            go(share_copy(p, d))
        go(pass_copy(p, 0))

    def forward(p, d):
        share_copy(p, d).wait_recv()
        go(pass_copy(p, d))

    def of_half(h):
        return range(h * per_half, (h + 1) * per_half)

    def gate_up(h, d):
        for p in of_half(h):
            pass_copy(p, d).wait_recv()
        i = lax.rem(x + n_x - d, n_x)
        span = pl.ds(h * hrows, hrows)
        held = jnp.concatenate([xbuf[i * 2, span], xbuf[i * 2 + 1, span]], axis=1)
        g_term = lax.dot_general(held, wg[i], NT, preferred_element_type=F32)
        act_g[h] = g_term if d == 0 else act_g[h] + g_term
        u_term = lax.dot_general(held, wu[i], NT, preferred_element_type=F32)
        act_u[h] = u_term if d == 0 else act_u[h] + u_term

    def pair_copy(q, d):
        i = lax.rem(x + d, n_x)
        return remote(
            part.at[q, 1 - c, i], peer.at[q, i], p_ss.at[q, d], p_rs.at[q, d],
            {"tensor": sibling_t},
        )

    targets = others[::-1] + (0,)

    def activate(h):
        g_all = act_g[h]
        hidden[...] = (g_all / (1.0 + jnp.exp(-g_all)) * act_u[h]).astype(BF16)

    def down(first, last):
        base = first % units_half
        held = hidden[base * urows : (base + last - first) * urows]
        for d in targets:
            i = lax.rem(x + d, n_x)
            o = jnp.dot(held, wd[i], preferred_element_type=F32).astype(BF16)
            for q in range(first, last):
                o_q = o[(q - first) * urows : (q - first + 1) * urows]
                part[q, 0, i] = o_q[:, :tcols]
                part[q, 1, i] = o_q[:, tcols:]
                go(pair_copy(q, d))

    def cross_copy(q, d):
        to = lax.rem(x + d, n_x)
        return remote(
            part.at[q, c, to], cross.at[q, d - 1], x_ss.at[q, d - 1], x_rs.at[q, d - 1],
            {"tensor": to * 2 + c},
        )

    def reduce_send(q):
        for d in targets:
            i = lax.rem(x + d, n_x)
            pair_copy(q, d).wait_recv()
            part[q, c, i] = (part[q, c, i].astype(F32) + peer[q, i].astype(F32)).astype(BF16)
            if d > 0:
                go(cross_copy(q, d))

    def return_copy(p):
        to = lax.rem(z + order[p], n_z)
        return remote(
            ybuf.at[p], zbuf.at[pl.ds(p * CAP, CAP)], z_ss.at[p], z_rs.at[p], {"expert": to}
        )

    def reduce_recv(q):
        total = part[q, c, x].astype(F32)
        for d in near + others[len(near) :]:
            cross_copy(q, d).wait_recv()
            total = total + cross[q, d - 1].astype(F32)
        total = total.astype(BF16)
        for i in range(per_unit)[::-1]:
            p = q * per_unit + i
            block = total[i * CAP : (i + 1) * CAP]
            if p == 0:
                zbuf[0:CAP] = block
            else:
                ybuf[p] = block
                go(return_copy(p))

    for p in range(1, min(3, n_z)):
        pick(p)
    pick(0)
    share(0)
    for p in range(3, n_z):
        pick(p)
    for load in loads:
        load.wait()
    for p in range(1, n_z):
        share(p)
    gate_up(0, 0)
    for d in near:
        for p in of_half(0):
            forward(p, d)
    gate_up(1, 0)
    for d in near:
        gate_up(0, d)
    for d in others[len(near) :]:
        for p in of_half(0):
            forward(p, d)
        gate_up(0, d)
    activate(0)
    down(0, units_half)
    for d in near:
        for p in of_half(1):
            forward(p, d)
    for q in range(units_half)[::-1]:
        reduce_send(q)
    for d in near:
        gate_up(1, d)
    for d in others[len(near) :]:
        for p in of_half(1):
            forward(p, d)
        gate_up(1, d)
    activate(1)
    for q in range(units_half, n_units)[::-1]:
        down(q, q + 1)
        reduce_send(q)
    for q in range(units_half)[::-1]:
        reduce_recv(q)
    for d in range(1, n_t):
        logit_copy(d).wait_recv()
    gates = jnp.transpose(logit_ref[...].reshape(rows, 128))[0:n_e]
    gates = 1.0 / (1.0 + jnp.exp(-gates))
    pieces = []
    for p in range(n_z):
        e = lax.rem(z + n_z - order[p], n_z)
        gate = jnp.where(expert == e, gates, 0.0)
        gate = jnp.sum(gate, axis=0, keepdims=True)
        pieces.append(jnp.where(table[pl.ds(e, 1), :] == slot, gate, 0.0))
    comb = jnp.transpose(jnp.concatenate(pieces, axis=0))
    high = comb.astype(BF16)
    comb_hi[...] = high
    comb_lo[...] = (comb - high.astype(F32)).astype(BF16)
    for q in range(units_half, n_units)[::-1]:
        reduce_recv(q)
    for p in range(1, n_z):
        return_copy(p).wait_recv()

    back = zbuf[...]
    mixture = jnp.dot(comb_hi[...], back, preferred_element_type=F32) + jnp.dot(
        comb_lo[...], back, preferred_element_type=F32
    )
    mix[...] = mixture.astype(BF16).reshape(n_t, trows, tcols)

    def final_copy(d):
        to = lax.rem(t + d, n_t)
        return remote(mix.at[to], fin.at[t], f_ss.at[d - 1], f_rs.at[d - 1], {"tensor": to})

    for d in range(1, n_t):
        go(final_copy(d))
    fin[t] = mix[t]
    for d in range(1, n_t):
        final_copy(d).wait_recv()
    for i in range(n_t):
        span = slice(i * tcols, (i + 1) * tcols)
        out_ref[:, span] = (mixed_ref[:, span] + fin[i].astype(F32)).astype(BF16)

    for copy in sent:
        copy.wait_send()


def slot_order(n_z):
    if n_z == 8:
        return (0, 1, 7, 2, 6, 3, 5, 4)
    return tuple(range(n_z))


def local(
    resid, queries, keys, values, out_weight, norm_gain, router_weight,
    gate_weight, up_weight, down_weight, expert_ids,
):
    n_y, n_z, n_t = lax.axis_size("dp"), lax.axis_size("expert"), lax.axis_size("tensor")
    n_x = n_t // 2
    rows, qcols = queries.shape[1], queries.shape[2]
    width = resid.shape[2]
    ff = gate_weight.shape[2]
    n_e = router_weight.shape[1]
    top = expert_ids.shape[2]
    ycols, tcols, trows, xcols = width // n_y, width // n_t, rows // n_t, width // n_x
    wcols = out_weight.shape[1]
    group = qcols // HEAD_WIDTH
    n_units = 4 if n_z % 4 == 0 else 2
    hrows, urows = n_z // 2 * CAP, n_z // n_units * CAP
    hbm = pl.BlockSpec(memory_space=pltpu.HBM)
    dma = pltpu.SemaphoreType.DMA
    V = pltpu.VMEM
    hops = n_z // 2

    out = pl.pallas_call(
        functools.partial(block_kernel, n_y, n_z, n_t, slot_order(n_z)),
        out_shape=jax.ShapeDtypeStruct((trows, width), BF16),
        in_specs=[hbm] * 11,
        out_specs=pl.BlockSpec(memory_space=pltpu.VMEM),
        scratch_shapes=[
            V((rows, qcols), BF16),
            V((1, width), F32),
            V((n_e, width), BF16),
            V((top, rows), jnp.int32),
            V((trows, width), F32),
            V((n_t, trows, tcols), BF16),
            V((n_t, trows, 128), F32),
            V((n_z, 2, rows, HEAD_WIDTH), BF16),
            V((n_z, wcols, qcols), BF16),
            V((n_z, qcols // HEAD_WIDTH, rows, rows), F32),
            V((n_y, group, rows, HEAD_WIDTH), BF16),
            V((2, n_y, n_x, trows, ycols), BF16),
            V((n_y, n_x, trows, ycols), BF16),
            V((n_x, n_y, trows, ycols), BF16),
            V((n_x - 1, n_y, trows, ycols), BF16),
            V((n_y, trows, ycols), BF16),
            V((n_y, trows, ycols), BF16),
            V((trows, width), BF16),
            V((n_t, trows, tcols), BF16),
            V((n_x, ff, xcols), BF16),
            V((n_x, ff, xcols), BF16),
            V((n_x, ff, xcols), BF16),
            V((n_z, CAP, tcols), BF16),
            V((n_t, n_z * CAP, tcols), BF16),
            V((n_e, rows), jnp.int32),
            V((hrows, ff), BF16),
            V((2, hrows, ff), F32),
            V((2, hrows, ff), F32),
            V((n_units, 2, n_x, urows, tcols), BF16),
            V((n_units, n_x, urows, tcols), BF16),
            V((n_units, n_x - 1, urows, tcols), BF16),
            V((n_z, CAP, tcols), BF16),
            V((n_z * CAP, tcols), BF16),
            V((rows, n_z * CAP), BF16),
            V((rows, n_z * CAP), BF16),
            V((n_t, trows, tcols), BF16),
            V((n_t, trows, tcols), BF16),
            dma((7,)), dma,
            dma((2, hops)), dma((2, hops)), dma((2, hops)), dma((2, hops)),
            dma((n_y - 1, group)), dma((n_y - 1, group)), dma((n_y,)), dma((n_y,)),
            dma((n_x - 1, n_y)), dma((n_x - 1, n_y)), dma((n_y - 1,)), dma((n_y - 1,)),
            dma((n_t - 1,)), dma((n_t - 1,)), dma((n_t - 1,)), dma((n_t - 1,)),
            dma((3, n_x)),
            dma((n_z,)), dma((n_z,)),
            dma((n_z, n_x - 1)), dma((n_z, n_x - 1)), dma((n_z, n_x)), dma((n_z, n_x)),
            dma((n_units, n_x)), dma((n_units, n_x)),
            dma((n_units, n_x - 1)), dma((n_units, n_x - 1)),
            dma((n_z,)), dma((n_z,)), dma((n_t - 1,)), dma((n_t - 1,)),
        ],
        compiler_params=pltpu.CompilerParams(
            collective_id=0, has_side_effects=True, vmem_limit_bytes=58 * 2**20
        ),
    )(
        queries[0], keys[0], values[0], out_weight.T, resid[0], norm_gain[None],
        router_weight.T, expert_ids[0].T,
        jnp.swapaxes(gate_weight, 1, 2)[0], jnp.swapaxes(up_weight, 1, 2)[0], down_weight[0],
    )
    return out[None]


def solution(mesh):
    return jax.shard_map(
        local,
        mesh=mesh,
        in_specs=(
            P("dp", "expert", None),
            P("dp", "expert", "tensor"),
            P("dp", "expert", "tensor"),
            P("dp", "expert", "tensor"),
            P("tensor", ("dp", "expert")),
            P(),
            P(),
            P("expert", None, "tensor"),
            P("expert", None, "tensor"),
            P("expert", "tensor", None),
            P("dp", "expert", None),
        ),
        out_specs=P("dp", ("expert", "tensor"), None),
        check_vma=False,
    )
```

```python
import functools

import jax
import jax.numpy as jnp
from jax import lax
from jax.experimental import pallas as pl
from jax.experimental.pallas import tpu as pltpu
from jax.sharding import PartitionSpec as P

HEAD_WIDTH = 128
CAP = 80
MESH = pl.DeviceIdType.MESH
F32 = jnp.float32
BF16 = jnp.bfloat16
NT = (((1,), (1,)), ((), ()))


def remote(src, dst, send_sem, recv_sem, device):
    return pltpu.make_async_remote_copy(
        src_ref=src,
        dst_ref=dst,
        send_sem=send_sem,
        recv_sem=recv_sem,
        device_id=device,
        device_id_type=MESH,
    )


def greet(devices):
    barrier = pltpu.get_barrier_semaphore()
    for device in devices:
        pl.semaphore_signal(barrier, inc=1, device_id=device, device_id_type=MESH)
    pl.semaphore_wait(barrier, len(devices))


def block_kernel(
    n_y, n_z, n_t, order,
    q_hbm, k_ref, v_ref, w_ref, resid_ref, gain_hbm, router_hbm, ids_hbm, wg_ref, wu_ref, wd_ref,
    out_ref,
    q_ref, gain_ref, router_ref, ids_ref, mixed_ref, cols_ref, logit_ref,
    kv, w, heads, a_part, a_peer, a_sums, a_cross, att, attn, res, sendn,
    wg, wu, wd, slots, xbuf, table, hidden, act_g, act_u, part, peer, cross, ybuf, zbuf, mix, fin,
    in_sem, res_sem,
    kv_ss, kv_rs, w_ss, w_rs, h_ss, h_rs, ap_ss, ap_rs, ax_ss, ax_rs, y_ss, y_rs,
    n_ss, n_rs, l_ss, l_rs,
    wsem, s_ss, s_rs, a_ss, a_rs, b_ss, b_rs, p_ss, p_rs, x_ss, x_rs, z_ss, z_rs, f_ss, f_rs,
):
    n_x = n_t // 2
    y, z, t = lax.axis_index("dp"), lax.axis_index("expert"), lax.axis_index("tensor")
    x, c = lax.div(t, 2), lax.rem(t, 2)
    right, left = lax.rem(z + 1, n_z), lax.rem(z + n_z - 1, n_z)
    rows = q_ref.shape[0]
    group = q_ref.shape[1] // HEAD_WIDTH
    width = mixed_ref.shape[1]
    ycols, tcols, trows, xcols = width // n_y, width // n_t, rows // n_t, width // n_x
    per = n_t // n_y
    half = w_ref.shape[0] // 2
    halves = 2
    per_half = n_z // halves
    n_units = 4 if n_z % 4 == 0 else 2
    per_unit = n_z // n_units
    units_half = n_units // halves
    hrows, urows = per_half * CAP, per_unit * CAP
    near = (1, n_x - 1) if n_x > 2 else (1,)
    others = near + ((2,) if n_x > 2 else ())
    sibling_t = t + 1 - 2 * c
    sent = []

    def go(copy):
        copy.start()
        sent.append(copy)

    res_copy = pltpu.make_async_copy(
        resid_ref.at[pl.ds(pl.multiple_of(t * trows, trows), trows)], res, res_sem
    )
    first = [
        pltpu.make_async_copy(k_ref, kv.at[z, 0], in_sem.at[0]),
        pltpu.make_async_copy(v_ref, kv.at[z, 1], in_sem.at[1]),
        pltpu.make_async_copy(w_ref, w.at[z], in_sem.at[2]),
        pltpu.make_async_copy(q_hbm, q_ref, in_sem.at[3]),
    ]
    later = [
        pltpu.make_async_copy(gain_hbm, gain_ref, in_sem.at[4]),
        pltpu.make_async_copy(router_hbm, router_ref, in_sem.at[5]),
        pltpu.make_async_copy(ids_hbm, ids_ref, in_sem.at[6]),
        res_copy,
    ]
    for copy in first + later:
        copy.start()
    greet(
        [{"expert": lax.rem(z + d, n_z)} for d in range(1, n_z)]
        + [{"dp": lax.rem(y + d, n_y)} for d in range(1, n_y)]
        + [{"tensor": lax.rem(t + d, n_t)} for d in range(1, n_t)]
    )
    for copy in first:
        copy.wait()
    loads = []
    for i in range(n_x):
        span = pl.ds(i * xcols, xcols)
        loads.append(pltpu.make_async_copy(wg_ref.at[:, span], wg.at[i], wsem.at[0, i]))
        loads.append(pltpu.make_async_copy(wu_ref.at[:, span], wu.at[i], wsem.at[1, i]))
    for i in range(n_x):
        span = pl.ds(i * xcols, xcols)
        loads.append(pltpu.make_async_copy(wd_ref.at[:, span], wd.at[i], wsem.at[2, i]))
    for load in loads:
        load.start()

    hops = n_z // 2

    def hop(way, s, piece):
        block = lax.rem(z + (n_z - s if way == 0 else s), n_z)
        if piece < 2:
            ref, sems = kv.at[block, piece], (kv_ss, kv_rs)
        else:
            ref, sems = w.at[block, pl.ds((piece - 2) * half, half)], (w_ss, w_rs)
        return remote(
            ref, ref, sems[0].at[way, s, piece % 2], sems[1].at[way, s, piece % 2],
            {"expert": right if way == 0 else left},
        )

    inside = lax.broadcasted_iota(jnp.int32, (rows, rows), 1) <= lax.broadcasted_iota(
        jnp.int32, (rows, rows), 0
    )
    state = {}

    def attend(blocks):
        keys = jnp.concatenate([kv[b, 0] for b in blocks], axis=0)
        vals = jnp.concatenate([kv[b, 1] for b in blocks], axis=0)
        for h in range(group):
            s_h = lax.dot_general(
                q_ref[:, h * HEAD_WIDTH : (h + 1) * HEAD_WIDTH], keys, NT,
                preferred_element_type=F32,
            ) * HEAD_WIDTH ** (-0.5)
            if h not in state:
                s_h = jnp.where(inside, s_h, -jnp.inf)
            else:
                s_h = jnp.concatenate(
                    [
                        s_h[:, k * rows : (k + 1) * rows] + jnp.where(b < z, 0.0, -jnp.inf)
                        for k, b in enumerate(blocks)
                    ],
                    axis=1,
                )
            top_h = jnp.max(s_h, axis=1, keepdims=True)
            if h in state:
                top_h = jnp.maximum(top_h, state[h][0])
            e_h = jnp.exp(s_h - top_h)
            sum_h = jnp.sum(e_h, axis=1, keepdims=True)
            o_h = jnp.dot(e_h.astype(BF16), vals, preferred_element_type=F32)
            if h in state:
                shrink = jnp.exp(state[h][0] - top_h)
                sum_h = sum_h + state[h][1] * shrink
                o_h = o_h + state[h][2] * shrink
            state[h] = (top_h, sum_h, o_h)

    for s in range(hops):
        for piece in range(4):
            for way in range(2):
                if s > 0:
                    hop(way, s - 1, piece).wait_recv()
                if s < hops - 1 or piece % 2 == way:
                    go(hop(way, s, piece))
        attend([z] if s == 0 else [lax.rem(z + n_z - s, n_z), lax.rem(z + s, n_z)])
    for way in range(2):
        hop(way, hops - 1, way).wait_recv()
    attend([lax.rem(z + hops, n_z)])

    turns = [0] + sorted(range(1, n_y), key=lambda d: min(d, n_y - d))

    def heads_copy(d, h):
        return remote(
            heads.at[y, h], heads.at[y, h], h_ss.at[d - 1, h], h_rs.at[d - 1, h],
            {"dp": lax.rem(y + d, n_y)},
        )

    for h in range(group):
        o_h = state[h][2] * (1.0 / state[h][1])
        heads[y, h] = o_h.astype(BF16)
        for d in turns[:0:-1]:
            go(heads_copy(d, h))
    for way in range(2):
        hop(way, hops - 1, 2 + way).wait_recv()

    sibling = {"tensor": t + 1 - 2 * c}
    w_all = w[...].reshape(ycols, w.shape[2])

    def head_pair(j):
        g = lax.rem(y + n_y - j, n_y)
        return remote(a_part.at[1 - c, g], a_peer.at[g], ap_ss.at[j], ap_rs.at[j], sibling)

    def head_cross(d, j):
        to = lax.rem(x + d, n_x)
        g = lax.rem(y + n_y - j, n_y)
        return remote(
            a_sums.at[to, g], a_cross.at[d - 1, g], ax_ss.at[d - 1, j], ax_rs.at[d - 1, j],
            {"tensor": to * 2 + c},
        )

    def head_sum(j):
        g = lax.rem(y + n_y - j, n_y)
        head_pair(j).wait_recv()
        a_sums[:, g] = (a_part[c, g].astype(F32) + a_peer[g].astype(F32)).astype(BF16)
        for d in others[::-1]:
            go(head_cross(d, j))

    for k, j in enumerate(turns):
        g = lax.rem(y + n_y - j, n_y)
        if j > 0:
            for h in range(group):
                heads_copy(j, h).wait_recv()
        held = jnp.concatenate([heads[g, h] for h in range(group)], axis=1)
        pr = lax.dot_general(held, w_all, NT, preferred_element_type=F32)
        pr = pr.astype(BF16).reshape(n_x, 2, trows, ycols)
        a_part[0, g] = pr[:, 0]
        a_part[1, g] = pr[:, 1]
        go(head_pair(j))
        if k > 0:
            head_sum(turns[k - 1])
    head_sum(turns[-1])

    def back_copy(d):
        to = lax.rem(y + d, n_y)
        return remote(att.at[to], attn.at[y], y_ss.at[d - 1], y_rs.at[d - 1], {"dp": to})

    for j in turns:
        g = lax.rem(y + n_y - j, n_y)
        total = a_sums[x, g].astype(F32)
        for d in others:
            head_cross(d, j).wait_recv()
            total = total + a_cross[d - 1, g].astype(F32)
        if j == 0:
            attn[y] = total.astype(BF16)
        else:
            att[g] = total.astype(BF16)
            go(back_copy(n_y - j))
    for copy in later:
        copy.wait()
    for d in range(1, n_y):
        back_copy(d).wait_recv()

    mixed = []
    square = jnp.zeros((trows, 1), F32)
    for g in range(n_y):
        m_g = res[:, g * ycols : (g + 1) * ycols].astype(F32) + attn[g].astype(F32)
        mixed_ref[:, g * ycols : (g + 1) * ycols] = m_g
        square = square + jnp.sum(m_g * m_g, axis=1, keepdims=True)
        mixed.append(m_g)
    scale = lax.rsqrt(square * (1.0 / width) + 1e-05)
    def cols_copy(d):
        to = lax.rem(t + d, n_t)
        return remote(
            sendn.at[to], cols_ref.at[t], n_ss.at[d - 1], n_rs.at[d - 1], {"tensor": to}
        )

    def logit_copy(d):
        to = lax.rem(t + d, n_t)
        return remote(
            logit_ref.at[t], logit_ref.at[t], l_ss.at[d - 1], l_rs.at[d - 1], {"tensor": to}
        )

    normed = []
    for g in range(n_y):
        n_g = (mixed[g] * scale * gain_ref[:, g * ycols : (g + 1) * ycols]).astype(BF16)
        for i in range(per):
            sendn[g * per + i] = n_g[:, i * tcols : (i + 1) * tcols]
        normed.append(n_g)
    for d in range(1, n_t):
        go(cols_copy(d))
    cols_ref[t] = sendn[t]
    logits = None
    for g in range(n_y):
        term = lax.dot_general(
            normed[g],
            router_ref[:, g * ycols : (g + 1) * ycols],
            NT,
            preferred_element_type=F32,
        )
        logits = term if logits is None else logits + term
    lane = lax.broadcasted_iota(jnp.int32, (trows, 128), 1)
    wide = jnp.zeros((trows, 128), F32)
    for e in range(router_ref.shape[0]):
        wide = jnp.where(lane == e, logits[:, e : e + 1], wide)
    logit_ref[t] = wide
    for d in range(1, n_t):
        go(logit_copy(d))

    n_e = table.shape[0]
    expert = lax.broadcasted_iota(jnp.int32, (n_e, rows), 0)
    ids = ids_ref[...]
    named = ids[0:1, :] == expert
    for j in range(1, ids.shape[0]):
        named = jnp.logical_or(named, ids[j : j + 1, :] == expert)
    earlier = (
        lax.broadcasted_iota(jnp.int32, (rows, rows), 0)
        < lax.broadcasted_iota(jnp.int32, (rows, rows), 1)
    )
    before = jnp.dot(
        jnp.where(named, 1.0, 0.0).astype(BF16),
        jnp.where(earlier, 1.0, 0.0).astype(BF16),
        preferred_element_type=F32,
    )
    table[...] = jnp.where(named, before.astype(jnp.int32), -1)
    for d in range(1, n_t):
        cols_copy(d).wait_recv()

    slot = lax.broadcasted_iota(jnp.int32, (CAP, rows), 0)
    cols = cols_ref[...].reshape(rows, tcols)

    def chunk(held, p):
        return xbuf.at[held, pl.ds(p * CAP, CAP)]

    def slot_copy(p):
        to = lax.rem(z + n_z - order[p], n_z)
        return remote(slots.at[p], chunk(t, p), s_ss.at[p], s_rs.at[p], {"expert": to})

    def pick(p):
        e = lax.rem(z + n_z - order[p], n_z)
        hot = jnp.where(table[pl.ds(e, 1), :] == slot, 1.0, 0.0).astype(BF16)
        picked = jnp.dot(hot, cols, preferred_element_type=F32).astype(BF16)
        if p == 0:
            xbuf[t, 0:CAP] = picked
        else:
            slots[p] = picked
            go(slot_copy(p))

    def share_copy(p, d):
        ref = chunk(t, p)
        to = lax.rem(x + d, n_x) * 2 + c
        return remote(ref, ref, a_ss.at[p, d - 1], a_rs.at[p, d - 1], {"tensor": to})

    def pass_copy(p, d):
        ref = chunk(lax.rem(x + n_x - d, n_x) * 2 + c, p)
        return remote(ref, ref, b_ss.at[p, d], b_rs.at[p, d], {"tensor": sibling_t})

    def share(p):
        if p > 0:
            slot_copy(p).wait_recv()
        for d in others[::-1]:
            go(share_copy(p, d))
        go(pass_copy(p, 0))

    def forward(p, d):
        share_copy(p, d).wait_recv()
        go(pass_copy(p, d))

    def of_half(h):
        return range(h * per_half, (h + 1) * per_half)

    def gate_up(h, d):
        for p in of_half(h):
            pass_copy(p, d).wait_recv()
        i = lax.rem(x + n_x - d, n_x)
        span = pl.ds(h * hrows, hrows)
        held = jnp.concatenate([xbuf[i * 2, span], xbuf[i * 2 + 1, span]], axis=1)
        g_term = lax.dot_general(held, wg[i], NT, preferred_element_type=F32)
        act_g[h] = g_term if d == 0 else act_g[h] + g_term
        u_term = lax.dot_general(held, wu[i], NT, preferred_element_type=F32)
        act_u[h] = u_term if d == 0 else act_u[h] + u_term

    def pair_copy(q, d):
        i = lax.rem(x + d, n_x)
        return remote(
            part.at[q, 1 - c, i], peer.at[q, i], p_ss.at[q, d], p_rs.at[q, d],
            {"tensor": sibling_t},
        )

    targets = others[::-1] + (0,)

    def activate(h):
        g_all = act_g[h]
        hidden[...] = (g_all / (1.0 + jnp.exp(-g_all)) * act_u[h]).astype(BF16)

    def down(first, last):
        base = first % units_half
        held = hidden[base * urows : (base + last - first) * urows]
        for d in targets:
            i = lax.rem(x + d, n_x)
            o = jnp.dot(held, wd[i], preferred_element_type=F32).astype(BF16)
            for q in range(first, last):
                o_q = o[(q - first) * urows : (q - first + 1) * urows]
                part[q, 0, i] = o_q[:, :tcols]
                part[q, 1, i] = o_q[:, tcols:]
                go(pair_copy(q, d))

    def cross_copy(q, d):
        to = lax.rem(x + d, n_x)
        return remote(
            part.at[q, c, to], cross.at[q, d - 1], x_ss.at[q, d - 1], x_rs.at[q, d - 1],
            {"tensor": to * 2 + c},
        )

    def reduce_send(q):
        for d in targets:
            i = lax.rem(x + d, n_x)
            pair_copy(q, d).wait_recv()
            part[q, c, i] = (part[q, c, i].astype(F32) + peer[q, i].astype(F32)).astype(BF16)
            if d > 0:
                go(cross_copy(q, d))

    def return_copy(p):
        to = lax.rem(z + order[p], n_z)
        return remote(
            ybuf.at[p], zbuf.at[pl.ds(p * CAP, CAP)], z_ss.at[p], z_rs.at[p], {"expert": to}
        )

    def reduce_recv(q):
        total = part[q, c, x].astype(F32)
        for d in near + others[len(near) :]:
            cross_copy(q, d).wait_recv()
            total = total + cross[q, d - 1].astype(F32)
        total = total.astype(BF16)
        for i in range(per_unit)[::-1]:
            p = q * per_unit + i
            block = total[i * CAP : (i + 1) * CAP]
            if p == 0:
                zbuf[0:CAP] = block
            else:
                ybuf[p] = block
                go(return_copy(p))

    for p in range(1, min(3, n_z)):
        pick(p)
    pick(0)
    share(0)
    for p in range(3, n_z):
        pick(p)
    for load in loads:
        load.wait()
    for p in range(1, n_z):
        share(p)
    gate_up(0, 0)
    for d in near:
        for p in of_half(0):
            forward(p, d)
    gate_up(1, 0)
    for d in near:
        gate_up(0, d)
    for d in others[len(near) :]:
        for p in of_half(0):
            forward(p, d)
        gate_up(0, d)
    activate(0)
    down(0, units_half)
    for d in near:
        for p in of_half(1):
            forward(p, d)
    for q in range(units_half)[::-1]:
        reduce_send(q)
    for d in near:
        gate_up(1, d)
    for d in others[len(near) :]:
        for p in of_half(1):
            forward(p, d)
        gate_up(1, d)
    activate(1)
    for q in range(units_half, n_units)[::-1]:
        down(q, q + 1)
        reduce_send(q)
    for q in range(units_half)[::-1]:
        reduce_recv(q)
    for d in range(1, n_t):
        logit_copy(d).wait_recv()
    gates = jnp.transpose(logit_ref[...].reshape(rows, 128))[0:n_e]
    gates = 1.0 / (1.0 + jnp.exp(-gates))
    pieces = []
    for p in range(n_z):
        e = lax.rem(z + n_z - order[p], n_z)
        gate = jnp.where(expert == e, gates, 0.0)
        gate = jnp.sum(gate, axis=0, keepdims=True)
        pieces.append(jnp.where(table[pl.ds(e, 1), :] == slot, gate, 0.0))
    combine = jnp.concatenate(pieces, axis=0)
    for q in range(units_half, n_units)[::-1]:
        reduce_recv(q)
    mixture = jnp.zeros((rows, tcols), F32)
    for first, last in [(0, units_half)] + [(q, q + 1) for q in range(units_half, n_units)[::-1]]:
        for p in range(first * per_unit, last * per_unit):
            if p > 0:
                return_copy(p).wait_recv()
        span = slice(first * urows, last * urows)
        back = zbuf[span]
        weights = combine[span]
        high = weights.astype(BF16)
        low = (weights - high.astype(F32)).astype(BF16)
        for term in (high, low):
            mixture = mixture + lax.dot_general(
                term, back, (((0,), (0,)), ((), ())), preferred_element_type=F32
            )
    mix[...] = mixture.astype(BF16).reshape(n_t, trows, tcols)

    def final_copy(d):
        to = lax.rem(t + d, n_t)
        return remote(mix.at[to], fin.at[t], f_ss.at[d - 1], f_rs.at[d - 1], {"tensor": to})

    for d in range(1, n_t):
        go(final_copy(d))
    fin[t] = mix[t]
    for d in range(1, n_t):
        final_copy(d).wait_recv()
    for i in range(n_t):
        span = slice(i * tcols, (i + 1) * tcols)
        out_ref[i] = (mixed_ref[:, span] + fin[i].astype(F32)).astype(BF16)

    for copy in sent:
        copy.wait_send()


def slot_order(n_z):
    if n_z == 8:
        return (0, 1, 7, 2, 6, 3, 5, 4)
    return tuple(range(n_z))


def local(
    resid, queries, keys, values, out_weight, norm_gain, router_weight,
    gate_weight, up_weight, down_weight, expert_ids,
):
    n_y, n_z, n_t = lax.axis_size("dp"), lax.axis_size("expert"), lax.axis_size("tensor")
    n_x = n_t // 2
    rows, qcols = queries.shape[1], queries.shape[2]
    width = resid.shape[2]
    ff = gate_weight.shape[2]
    n_e = router_weight.shape[1]
    top = expert_ids.shape[2]
    ycols, tcols, trows, xcols = width // n_y, width // n_t, rows // n_t, width // n_x
    wcols = out_weight.shape[1]
    group = qcols // HEAD_WIDTH
    n_units = 4 if n_z % 4 == 0 else 2
    hrows, urows = n_z // 2 * CAP, n_z // n_units * CAP
    hbm = pl.BlockSpec(memory_space=pltpu.HBM)
    dma = pltpu.SemaphoreType.DMA
    V = pltpu.VMEM
    hops = n_z // 2

    out = pl.pallas_call(
        functools.partial(block_kernel, n_y, n_z, n_t, slot_order(n_z)),
        out_shape=jax.ShapeDtypeStruct((n_t, trows, tcols), BF16),
        in_specs=[hbm] * 11,
        out_specs=pl.BlockSpec(memory_space=pltpu.VMEM),
        scratch_shapes=[
            V((rows, qcols), BF16),
            V((1, width), F32),
            V((n_e, width), BF16),
            V((top, rows), jnp.int32),
            V((trows, width), F32),
            V((n_t, trows, tcols), BF16),
            V((n_t, trows, 128), F32),
            V((n_z, 2, rows, HEAD_WIDTH), BF16),
            V((n_z, wcols, qcols), BF16),
            V((n_y, group, rows, HEAD_WIDTH), BF16),
            V((2, n_y, n_x, trows, ycols), BF16),
            V((n_y, n_x, trows, ycols), BF16),
            V((n_x, n_y, trows, ycols), BF16),
            V((n_x - 1, n_y, trows, ycols), BF16),
            V((n_y, trows, ycols), BF16),
            V((n_y, trows, ycols), BF16),
            V((trows, width), BF16),
            V((n_t, trows, tcols), BF16),
            V((n_x, ff, xcols), BF16),
            V((n_x, ff, xcols), BF16),
            V((n_x, ff, xcols), BF16),
            V((n_z, CAP, tcols), BF16),
            V((n_t, n_z * CAP, tcols), BF16),
            V((n_e, rows), jnp.int32),
            V((hrows, ff), BF16),
            V((2, hrows, ff), F32),
            V((2, hrows, ff), F32),
            V((n_units, 2, n_x, urows, tcols), BF16),
            V((n_units, n_x, urows, tcols), BF16),
            V((n_units, n_x - 1, urows, tcols), BF16),
            V((n_z, CAP, tcols), BF16),
            V((n_z * CAP, tcols), BF16),
            V((n_t, trows, tcols), BF16),
            V((n_t, trows, tcols), BF16),
            dma((7,)), dma,
            dma((2, hops, 2)), dma((2, hops, 2)), dma((2, hops, 2)), dma((2, hops, 2)),
            dma((n_y - 1, group)), dma((n_y - 1, group)), dma((n_y,)), dma((n_y,)),
            dma((n_x - 1, n_y)), dma((n_x - 1, n_y)), dma((n_y - 1,)), dma((n_y - 1,)),
            dma((n_t - 1,)), dma((n_t - 1,)), dma((n_t - 1,)), dma((n_t - 1,)),
            dma((3, n_x)),
            dma((n_z,)), dma((n_z,)),
            dma((n_z, n_x - 1)), dma((n_z, n_x - 1)), dma((n_z, n_x)), dma((n_z, n_x)),
            dma((n_units, n_x)), dma((n_units, n_x)),
            dma((n_units, n_x - 1)), dma((n_units, n_x - 1)),
            dma((n_z,)), dma((n_z,)), dma((n_t - 1,)), dma((n_t - 1,)),
        ],
        compiler_params=pltpu.CompilerParams(
            collective_id=0, has_side_effects=True, vmem_limit_bytes=58 * 2**20
        ),
    )(
        queries[0], keys[0], values[0], out_weight.T, resid[0], norm_gain[None],
        router_weight.T, expert_ids[0].T,
        jnp.swapaxes(gate_weight, 1, 2)[0], jnp.swapaxes(up_weight, 1, 2)[0], down_weight[0],
    )
    return jnp.swapaxes(out, 0, 1).reshape(1, trows, width)


def solution(mesh):
    return jax.shard_map(
        local,
        mesh=mesh,
        in_specs=(
            P("dp", "expert", None),
            P("dp", "expert", "tensor"),
            P("dp", "expert", "tensor"),
            P("dp", "expert", "tensor"),
            P("tensor", ("dp", "expert")),
            P(),
            P(),
            P("expert", None, "tensor"),
            P("expert", None, "tensor"),
            P("expert", "tensor", None),
            P("dp", "expert", None),
        ),
        out_specs=P("dp", ("expert", "tensor"), None),
        check_vma=False,
    )
```

```python
import functools

import jax
import jax.numpy as jnp
from jax import lax
from jax.experimental import pallas as pl
from jax.experimental.pallas import tpu as pltpu
from jax.sharding import PartitionSpec as P

HEAD_WIDTH = 128
CAP = 80
MESH = pl.DeviceIdType.MESH
F32 = jnp.float32
BF16 = jnp.bfloat16
NT = (((1,), (1,)), ((), ()))


def remote(src, dst, send_sem, recv_sem, device):
    return pltpu.make_async_remote_copy(
        src_ref=src,
        dst_ref=dst,
        send_sem=send_sem,
        recv_sem=recv_sem,
        device_id=device,
        device_id_type=MESH,
    )


def greet(devices):
    barrier = pltpu.get_barrier_semaphore()
    for device in devices:
        pl.semaphore_signal(barrier, inc=1, device_id=device, device_id_type=MESH)
    pl.semaphore_wait(barrier, len(devices))


def block_kernel(
    n_y, n_z, n_t, order,
    q_hbm, k_ref, v_ref, w_ref, resid_ref, gain_hbm, router_hbm, ids_hbm, wg_ref, wu_ref, wd_ref,
    out_ref,
    q_ref, gain_ref, router_ref, ids_ref, mixed_ref, cols_ref, logit_ref,
    kv, w, heads, a_part, a_peer, a_sums, a_cross, att, attn, res, sendn,
    wg, wu, wd, slots, xbuf, table, hidden, act_g, act_u, part, peer, cross, ybuf, zbuf, mix, fin,
    in_sem, res_sem,
    kv_ss, kv_rs, w_ss, w_rs, h_ss, h_rs, ap_ss, ap_rs, ax_ss, ax_rs, y_ss, y_rs,
    n_ss, n_rs, l_ss, l_rs,
    wsem, s_ss, s_rs, a_ss, a_rs, b_ss, b_rs, p_ss, p_rs, x_ss, x_rs, z_ss, z_rs, f_ss, f_rs,
):
    n_x = n_t // 2
    y, z, t = lax.axis_index("dp"), lax.axis_index("expert"), lax.axis_index("tensor")
    x, c = lax.div(t, 2), lax.rem(t, 2)
    right, left = lax.rem(z + 1, n_z), lax.rem(z + n_z - 1, n_z)
    rows = q_ref.shape[0]
    group = q_ref.shape[1] // HEAD_WIDTH
    width = mixed_ref.shape[1]
    ycols, tcols, trows, xcols = width // n_y, width // n_t, rows // n_t, width // n_x
    per = n_t // n_y
    half = w_ref.shape[0] // 2
    halves = 2
    per_half = n_z // halves
    n_units = 4 if n_z % 4 == 0 else 2
    per_unit = n_z // n_units
    units_half = n_units // halves
    hrows, urows = per_half * CAP, per_unit * CAP
    near = (1, n_x - 1) if n_x > 2 else (1,)
    others = near + ((2,) if n_x > 2 else ())
    sibling_t = t + 1 - 2 * c
    sent = []

    def go(copy):
        copy.start()
        sent.append(copy)

    res_copy = pltpu.make_async_copy(
        resid_ref.at[pl.ds(pl.multiple_of(t * trows, trows), trows)], res, res_sem
    )
    first = [
        pltpu.make_async_copy(k_ref, kv.at[z, 0], in_sem.at[0]),
        pltpu.make_async_copy(v_ref, kv.at[z, 1], in_sem.at[1]),
        pltpu.make_async_copy(w_ref, w.at[z], in_sem.at[2]),
        pltpu.make_async_copy(q_hbm, q_ref, in_sem.at[3]),
    ]
    later = [
        pltpu.make_async_copy(gain_hbm, gain_ref, in_sem.at[4]),
        pltpu.make_async_copy(router_hbm, router_ref, in_sem.at[5]),
        pltpu.make_async_copy(ids_hbm, ids_ref, in_sem.at[6]),
        res_copy,
    ]
    for copy in first + later:
        copy.start()
    greet(
        [{"expert": lax.rem(z + d, n_z)} for d in range(1, n_z)]
        + [{"dp": lax.rem(y + d, n_y)} for d in range(1, n_y)]
        + [{"tensor": lax.rem(t + d, n_t)} for d in range(1, n_t)]
    )
    for copy in first:
        copy.wait()
    loads = []
    for i in range(n_x):
        span = pl.ds(i * xcols, xcols)
        loads.append(pltpu.make_async_copy(wg_ref.at[:, span], wg.at[i], wsem.at[0, i]))
        loads.append(pltpu.make_async_copy(wu_ref.at[:, span], wu.at[i], wsem.at[1, i]))
    for i in range(n_x):
        span = pl.ds(i * xcols, xcols)
        loads.append(pltpu.make_async_copy(wd_ref.at[:, span], wd.at[i], wsem.at[2, i]))
    hops = n_z // 2

    def hop(way, s, piece):
        block = lax.rem(z + (n_z - s if way == 0 else s), n_z)
        if piece < 2:
            ref, sems = kv.at[block, piece], (kv_ss, kv_rs)
        else:
            ref, sems = w.at[block, pl.ds((piece - 2) * half, half)], (w_ss, w_rs)
        return remote(
            ref, ref, sems[0].at[way, s, piece % 2], sems[1].at[way, s, piece % 2],
            {"expert": right if way == 0 else left},
        )

    inside = lax.broadcasted_iota(jnp.int32, (rows, rows), 1) <= lax.broadcasted_iota(
        jnp.int32, (rows, rows), 0
    )
    state = {}

    def attend(blocks):
        keys = jnp.concatenate([kv[b, 0] for b in blocks], axis=0)
        vals = jnp.concatenate([kv[b, 1] for b in blocks], axis=0)
        for h in range(group):
            s_h = lax.dot_general(
                q_ref[:, h * HEAD_WIDTH : (h + 1) * HEAD_WIDTH], keys, NT,
                preferred_element_type=F32,
            ) * HEAD_WIDTH ** (-0.5)
            if h not in state:
                s_h = jnp.where(inside, s_h, -jnp.inf)
            else:
                s_h = jnp.concatenate(
                    [
                        s_h[:, k * rows : (k + 1) * rows] + jnp.where(b < z, 0.0, -jnp.inf)
                        for k, b in enumerate(blocks)
                    ],
                    axis=1,
                )
            top_h = jnp.max(s_h, axis=1, keepdims=True)
            if h in state:
                top_h = jnp.maximum(top_h, state[h][0])
            e_h = jnp.exp(s_h - top_h)
            sum_h = jnp.sum(e_h, axis=1, keepdims=True)
            o_h = jnp.dot(e_h.astype(BF16), vals, preferred_element_type=F32)
            if h in state:
                shrink = jnp.exp(state[h][0] - top_h)
                sum_h = sum_h + state[h][1] * shrink
                o_h = o_h + state[h][2] * shrink
            state[h] = (top_h, sum_h, o_h)

    for s in range(hops):
        for piece in range(4):
            for way in range(2):
                if s > 0:
                    hop(way, s - 1, piece).wait_recv()
                if s < hops - 1 or piece % 2 == way:
                    go(hop(way, s, piece))
        if s == 0:
            for load in loads:
                load.start()
        attend([z] if s == 0 else [lax.rem(z + n_z - s, n_z), lax.rem(z + s, n_z)])
    for way in range(2):
        hop(way, hops - 1, way).wait_recv()
    attend([lax.rem(z + hops, n_z)])

    turns = [0] + sorted(range(1, n_y), key=lambda d: min(d, n_y - d))

    def heads_copy(d, h):
        return remote(
            heads.at[y, h], heads.at[y, h], h_ss.at[d - 1, h], h_rs.at[d - 1, h],
            {"dp": lax.rem(y + d, n_y)},
        )

    for h in range(group):
        o_h = state[h][2] * (1.0 / state[h][1])
        heads[y, h] = o_h.astype(BF16)
        for d in turns[:0:-1]:
            go(heads_copy(d, h))
    for way in range(2):
        hop(way, hops - 1, 2 + way).wait_recv()

    sibling = {"tensor": t + 1 - 2 * c}
    w_all = w[...].reshape(ycols, w.shape[2])

    def head_pair(j):
        g = lax.rem(y + n_y - j, n_y)
        return remote(a_part.at[1 - c, g], a_peer.at[g], ap_ss.at[j], ap_rs.at[j], sibling)

    def head_cross(d, j):
        to = lax.rem(x + d, n_x)
        g = lax.rem(y + n_y - j, n_y)
        return remote(
            a_sums.at[to, g], a_cross.at[d - 1, g], ax_ss.at[d - 1, j], ax_rs.at[d - 1, j],
            {"tensor": to * 2 + c},
        )

    def head_sum(j):
        g = lax.rem(y + n_y - j, n_y)
        head_pair(j).wait_recv()
        a_sums[:, g] = (a_part[c, g].astype(F32) + a_peer[g].astype(F32)).astype(BF16)
        for d in others[::-1]:
            go(head_cross(d, j))

    for k, j in enumerate(turns):
        g = lax.rem(y + n_y - j, n_y)
        if j > 0:
            for h in range(group):
                heads_copy(j, h).wait_recv()
        held = jnp.concatenate([heads[g, h] for h in range(group)], axis=1)
        pr = lax.dot_general(held, w_all, NT, preferred_element_type=F32)
        pr = pr.astype(BF16).reshape(n_x, 2, trows, ycols)
        a_part[0, g] = pr[:, 0]
        a_part[1, g] = pr[:, 1]
        go(head_pair(j))
        if k > 0:
            head_sum(turns[k - 1])
    head_sum(turns[-1])

    def back_copy(d):
        to = lax.rem(y + d, n_y)
        return remote(att.at[to], attn.at[y], y_ss.at[d - 1], y_rs.at[d - 1], {"dp": to})

    for j in turns:
        g = lax.rem(y + n_y - j, n_y)
        total = a_sums[x, g].astype(F32)
        for d in others:
            head_cross(d, j).wait_recv()
            total = total + a_cross[d - 1, g].astype(F32)
        if j == 0:
            attn[y] = total.astype(BF16)
        else:
            att[g] = total.astype(BF16)
            go(back_copy(n_y - j))
    for copy in later:
        copy.wait()
    for d in range(1, n_y):
        back_copy(d).wait_recv()

    mixed = []
    square = jnp.zeros((trows, 1), F32)
    for g in range(n_y):
        m_g = res[:, g * ycols : (g + 1) * ycols].astype(F32) + attn[g].astype(F32)
        mixed_ref[:, g * ycols : (g + 1) * ycols] = m_g
        square = square + jnp.sum(m_g * m_g, axis=1, keepdims=True)
        mixed.append(m_g)
    scale = lax.rsqrt(square * (1.0 / width) + 1e-05)
    def cols_copy(d):
        to = lax.rem(t + d, n_t)
        return remote(
            sendn.at[to], cols_ref.at[t], n_ss.at[d - 1], n_rs.at[d - 1], {"tensor": to}
        )

    def logit_copy(d):
        to = lax.rem(t + d, n_t)
        return remote(
            logit_ref.at[t], logit_ref.at[t], l_ss.at[d - 1], l_rs.at[d - 1], {"tensor": to}
        )

    normed = []
    for g in range(n_y):
        n_g = (mixed[g] * scale * gain_ref[:, g * ycols : (g + 1) * ycols]).astype(BF16)
        for i in range(per):
            sendn[g * per + i] = n_g[:, i * tcols : (i + 1) * tcols]
        normed.append(n_g)
    for d in range(1, n_t):
        go(cols_copy(d))
    cols_ref[t] = sendn[t]
    logits = None
    for g in range(n_y):
        term = lax.dot_general(
            normed[g],
            router_ref[:, g * ycols : (g + 1) * ycols],
            NT,
            preferred_element_type=F32,
        )
        logits = term if logits is None else logits + term
    lane = lax.broadcasted_iota(jnp.int32, (trows, 128), 1)
    wide = jnp.zeros((trows, 128), F32)
    for e in range(router_ref.shape[0]):
        wide = jnp.where(lane == e, logits[:, e : e + 1], wide)
    logit_ref[t] = wide
    for d in range(1, n_t):
        go(logit_copy(d))

    n_e = table.shape[0]
    expert = lax.broadcasted_iota(jnp.int32, (n_e, rows), 0)
    ids = ids_ref[...]
    named = ids[0:1, :] == expert
    for j in range(1, ids.shape[0]):
        named = jnp.logical_or(named, ids[j : j + 1, :] == expert)
    earlier = (
        lax.broadcasted_iota(jnp.int32, (rows, rows), 0)
        < lax.broadcasted_iota(jnp.int32, (rows, rows), 1)
    )
    before = jnp.dot(
        jnp.where(named, 1.0, 0.0).astype(BF16),
        jnp.where(earlier, 1.0, 0.0).astype(BF16),
        preferred_element_type=F32,
    )
    table[...] = jnp.where(named, before.astype(jnp.int32), -1)
    for d in range(1, n_t):
        cols_copy(d).wait_recv()

    slot = lax.broadcasted_iota(jnp.int32, (CAP, rows), 0)
    cols = cols_ref[...].reshape(rows, tcols)

    def chunk(held, p):
        return xbuf.at[held, pl.ds(p * CAP, CAP)]

    def slot_copy(p):
        to = lax.rem(z + n_z - order[p], n_z)
        return remote(slots.at[p], chunk(t, p), s_ss.at[p], s_rs.at[p], {"expert": to})

    def pick(p):
        e = lax.rem(z + n_z - order[p], n_z)
        hot = jnp.where(table[pl.ds(e, 1), :] == slot, 1.0, 0.0).astype(BF16)
        picked = jnp.dot(hot, cols, preferred_element_type=F32).astype(BF16)
        if p == 0:
            xbuf[t, 0:CAP] = picked
        else:
            slots[p] = picked
            go(slot_copy(p))

    def share_copy(p, d):
        ref = chunk(t, p)
        to = lax.rem(x + d, n_x) * 2 + c
        return remote(ref, ref, a_ss.at[p, d - 1], a_rs.at[p, d - 1], {"tensor": to})

    def pass_copy(p, d):
        ref = chunk(lax.rem(x + n_x - d, n_x) * 2 + c, p)
        return remote(ref, ref, b_ss.at[p, d], b_rs.at[p, d], {"tensor": sibling_t})

    def share(p):
        if p > 0:
            slot_copy(p).wait_recv()
        for d in others[::-1]:
            go(share_copy(p, d))
        go(pass_copy(p, 0))

    def forward(p, d):
        share_copy(p, d).wait_recv()
        go(pass_copy(p, d))

    def of_half(h):
        return range(h * per_half, (h + 1) * per_half)

    def gate_up(h, d):
        for p in of_half(h):
            pass_copy(p, d).wait_recv()
        i = lax.rem(x + n_x - d, n_x)
        span = pl.ds(h * hrows, hrows)
        held = jnp.concatenate([xbuf[i * 2, span], xbuf[i * 2 + 1, span]], axis=1)
        g_term = lax.dot_general(held, wg[i], NT, preferred_element_type=F32)
        act_g[h] = g_term if d == 0 else act_g[h] + g_term
        u_term = lax.dot_general(held, wu[i], NT, preferred_element_type=F32)
        act_u[h] = u_term if d == 0 else act_u[h] + u_term

    def pair_copy(q, d):
        i = lax.rem(x + d, n_x)
        return remote(
            part.at[q, 1 - c, i], peer.at[q, i], p_ss.at[q, d], p_rs.at[q, d],
            {"tensor": sibling_t},
        )

    targets = others[::-1] + (0,)

    def activate(h):
        g_all = act_g[h]
        hidden[...] = (g_all / (1.0 + jnp.exp(-g_all)) * act_u[h]).astype(BF16)

    def down(first, last):
        base = first % units_half
        held = hidden[base * urows : (base + last - first) * urows]
        for d in targets:
            i = lax.rem(x + d, n_x)
            o = jnp.dot(held, wd[i], preferred_element_type=F32).astype(BF16)
            for q in range(first, last):
                o_q = o[(q - first) * urows : (q - first + 1) * urows]
                part[q, 0, i] = o_q[:, :tcols]
                part[q, 1, i] = o_q[:, tcols:]
                go(pair_copy(q, d))

    def cross_copy(q, d):
        to = lax.rem(x + d, n_x)
        return remote(
            part.at[q, c, to], cross.at[q, d - 1], x_ss.at[q, d - 1], x_rs.at[q, d - 1],
            {"tensor": to * 2 + c},
        )

    def reduce_send(q):
        for d in targets:
            i = lax.rem(x + d, n_x)
            pair_copy(q, d).wait_recv()
            part[q, c, i] = (part[q, c, i].astype(F32) + peer[q, i].astype(F32)).astype(BF16)
            if d > 0:
                go(cross_copy(q, d))

    def return_copy(p):
        to = lax.rem(z + order[p], n_z)
        return remote(
            ybuf.at[p], zbuf.at[pl.ds(p * CAP, CAP)], z_ss.at[p], z_rs.at[p], {"expert": to}
        )

    def reduce_recv(q):
        total = part[q, c, x].astype(F32)
        for d in near + others[len(near) :]:
            cross_copy(q, d).wait_recv()
            total = total + cross[q, d - 1].astype(F32)
        total = total.astype(BF16)
        for i in range(per_unit)[::-1]:
            p = q * per_unit + i
            block = total[i * CAP : (i + 1) * CAP]
            if p == 0:
                zbuf[0:CAP] = block
            else:
                ybuf[p] = block
                go(return_copy(p))

    for p in range(1, min(3, n_z)):
        pick(p)
    pick(0)
    share(0)
    for p in range(3, n_z):
        pick(p)
    for load in loads:
        load.wait()
    for p in range(1, n_z):
        share(p)
    gate_up(0, 0)
    for d in near:
        for p in of_half(0):
            forward(p, d)
    gate_up(1, 0)
    for d in near:
        gate_up(0, d)
    for d in others[len(near) :]:
        for p in of_half(0):
            forward(p, d)
        gate_up(0, d)
    activate(0)
    down(0, units_half)
    for d in near:
        for p in of_half(1):
            forward(p, d)
    for q in range(units_half)[::-1]:
        reduce_send(q)
    for d in near:
        gate_up(1, d)
    for d in others[len(near) :]:
        for p in of_half(1):
            forward(p, d)
        gate_up(1, d)
    activate(1)
    for q in range(units_half, n_units)[::-1]:
        down(q, q + 1)
        reduce_send(q)
    for q in range(units_half)[::-1]:
        reduce_recv(q)
    for d in range(1, n_t):
        logit_copy(d).wait_recv()
    gates = jnp.transpose(logit_ref[...].reshape(rows, 128))[0:n_e]
    gates = 1.0 / (1.0 + jnp.exp(-gates))
    pieces = []
    for p in range(n_z):
        e = lax.rem(z + n_z - order[p], n_z)
        gate = jnp.where(expert == e, gates, 0.0)
        gate = jnp.sum(gate, axis=0, keepdims=True)
        pieces.append(jnp.where(table[pl.ds(e, 1), :] == slot, gate, 0.0))
    combine = jnp.concatenate(pieces, axis=0)
    for q in range(units_half, n_units)[::-1]:
        reduce_recv(q)
    mixture = jnp.zeros((rows, tcols), F32)
    for first, last in [(0, units_half)] + [(q, q + 1) for q in range(units_half, n_units)[::-1]]:
        for p in range(first * per_unit, last * per_unit):
            if p > 0:
                return_copy(p).wait_recv()
        span = slice(first * urows, last * urows)
        back = zbuf[span]
        weights = combine[span]
        high = weights.astype(BF16)
        low = (weights - high.astype(F32)).astype(BF16)
        for term in (high, low):
            mixture = mixture + lax.dot_general(
                term, back, (((0,), (0,)), ((), ())), preferred_element_type=F32
            )
    mix[...] = mixture.astype(BF16).reshape(n_t, trows, tcols)

    def final_copy(d):
        to = lax.rem(t + d, n_t)
        return remote(mix.at[to], fin.at[t], f_ss.at[d - 1], f_rs.at[d - 1], {"tensor": to})

    for d in range(1, n_t):
        go(final_copy(d))
    fin[t] = mix[t]
    for d in range(1, n_t):
        final_copy(d).wait_recv()
    for i in range(n_t):
        span = slice(i * tcols, (i + 1) * tcols)
        out_ref[i] = (mixed_ref[:, span] + fin[i].astype(F32)).astype(BF16)

    for copy in sent:
        copy.wait_send()


def slot_order(n_z):
    if n_z == 8:
        return (0, 1, 7, 2, 6, 3, 5, 4)
    return tuple(range(n_z))


def local(
    resid, queries, keys, values, out_weight, norm_gain, router_weight,
    gate_weight, up_weight, down_weight, expert_ids,
):
    n_y, n_z, n_t = lax.axis_size("dp"), lax.axis_size("expert"), lax.axis_size("tensor")
    n_x = n_t // 2
    rows, qcols = queries.shape[1], queries.shape[2]
    width = resid.shape[2]
    ff = gate_weight.shape[2]
    n_e = router_weight.shape[1]
    top = expert_ids.shape[2]
    ycols, tcols, trows, xcols = width // n_y, width // n_t, rows // n_t, width // n_x
    wcols = out_weight.shape[1]
    group = qcols // HEAD_WIDTH
    n_units = 4 if n_z % 4 == 0 else 2
    hrows, urows = n_z // 2 * CAP, n_z // n_units * CAP
    hbm = pl.BlockSpec(memory_space=pltpu.HBM)
    dma = pltpu.SemaphoreType.DMA
    V = pltpu.VMEM
    hops = n_z // 2

    out = pl.pallas_call(
        functools.partial(block_kernel, n_y, n_z, n_t, slot_order(n_z)),
        out_shape=jax.ShapeDtypeStruct((n_t, trows, tcols), BF16),
        in_specs=[hbm] * 11,
        out_specs=pl.BlockSpec(memory_space=pltpu.VMEM),
        scratch_shapes=[
            V((rows, qcols), BF16),
            V((1, width), F32),
            V((n_e, width), BF16),
            V((top, rows), jnp.int32),
            V((trows, width), F32),
            V((n_t, trows, tcols), BF16),
            V((n_t, trows, 128), F32),
            V((n_z, 2, rows, HEAD_WIDTH), BF16),
            V((n_z, wcols, qcols), BF16),
            V((n_y, group, rows, HEAD_WIDTH), BF16),
            V((2, n_y, n_x, trows, ycols), BF16),
            V((n_y, n_x, trows, ycols), BF16),
            V((n_x, n_y, trows, ycols), BF16),
            V((n_x - 1, n_y, trows, ycols), BF16),
            V((n_y, trows, ycols), BF16),
            V((n_y, trows, ycols), BF16),
            V((trows, width), BF16),
            V((n_t, trows, tcols), BF16),
            V((n_x, ff, xcols), BF16),
            V((n_x, ff, xcols), BF16),
            V((n_x, ff, xcols), BF16),
            V((n_z, CAP, tcols), BF16),
            V((n_t, n_z * CAP, tcols), BF16),
            V((n_e, rows), jnp.int32),
            V((hrows, ff), BF16),
            V((2, hrows, ff), F32),
            V((2, hrows, ff), F32),
            V((n_units, 2, n_x, urows, tcols), BF16),
            V((n_units, n_x, urows, tcols), BF16),
            V((n_units, n_x - 1, urows, tcols), BF16),
            V((n_z, CAP, tcols), BF16),
            V((n_z * CAP, tcols), BF16),
            V((n_t, trows, tcols), BF16),
            V((n_t, trows, tcols), BF16),
            dma((7,)), dma,
            dma((2, hops, 2)), dma((2, hops, 2)), dma((2, hops, 2)), dma((2, hops, 2)),
            dma((n_y - 1, group)), dma((n_y - 1, group)), dma((n_y,)), dma((n_y,)),
            dma((n_x - 1, n_y)), dma((n_x - 1, n_y)), dma((n_y - 1,)), dma((n_y - 1,)),
            dma((n_t - 1,)), dma((n_t - 1,)), dma((n_t - 1,)), dma((n_t - 1,)),
            dma((3, n_x)),
            dma((n_z,)), dma((n_z,)),
            dma((n_z, n_x - 1)), dma((n_z, n_x - 1)), dma((n_z, n_x)), dma((n_z, n_x)),
            dma((n_units, n_x)), dma((n_units, n_x)),
            dma((n_units, n_x - 1)), dma((n_units, n_x - 1)),
            dma((n_z,)), dma((n_z,)), dma((n_t - 1,)), dma((n_t - 1,)),
        ],
        compiler_params=pltpu.CompilerParams(
            collective_id=0, has_side_effects=True, vmem_limit_bytes=58 * 2**20
        ),
    )(
        queries[0], keys[0], values[0], out_weight.T, resid[0], norm_gain[None],
        router_weight.T, expert_ids[0].T,
        jnp.swapaxes(gate_weight, 1, 2)[0], jnp.swapaxes(up_weight, 1, 2)[0], down_weight[0],
    )
    return jnp.swapaxes(out, 0, 1).reshape(1, trows, width)


def solution(mesh):
    return jax.shard_map(
        local,
        mesh=mesh,
        in_specs=(
            P("dp", "expert", None),
            P("dp", "expert", "tensor"),
            P("dp", "expert", "tensor"),
            P("dp", "expert", "tensor"),
            P("tensor", ("dp", "expert")),
            P(),
            P(),
            P("expert", None, "tensor"),
            P("expert", None, "tensor"),
            P("expert", "tensor", None),
            P("dp", "expert", None),
        ),
        out_specs=P("dp", ("expert", "tensor"), None),
        check_vma=False,
    )
```
